256 devices in a mesh: dp: 4 (over x), ex: 16 (over z, y_hi), ey: 4 (over y_lo, core).
Axes of the slice: x: 4, y: 4 (y_hi: 2, y_lo: 2; y = y_hi * 2 + y_lo), z: 8, core: 2. Of those that a mesh axis runs over, the one named last changes fastest.
Arguments:
- tokens: bfloat16 [2, 12288, 2048], P(None, ('dp', 'ex', 'ey')), parts along dimension 1, may hold values from -6 to 6
- expert_ids: int32 [2, 12288, 8], P(None, ('dp', 'ex', 'ey')), parts along dimension 1, may hold values from 0 to 63, as said below
- slot_ids: int32 [2, 12288, 8], P(None, ('dp', 'ex', 'ey')), parts along dimension 1, may hold values from -1 to 7, as said below
- gate_values: float32 [2, 12288, 8], P(None, ('dp', 'ex', 'ey')), parts along dimension 1, may hold values from 0.05 to 1
- gate_weight: bfloat16 [64, 2048, 1024], P(('ex', 'ey')), may hold values from -0.125 to 0.125
- up_weight: bfloat16 [64, 2048, 1024], P(('ex', 'ey')), may hold values from -0.125 to 0.125
- down_weight: bfloat16 [64, 1024, 2048], P(('ex', 'ey')), may hold values from -0.1875 to 0.1875
Outputs:
- mixture: bfloat16 [2, 12288, 2048], P(None, ('dp', 'ex', 'ey')), parts along dimension 1
The draws below stay inside these ranges and needn't reach their ends.
There are 4 independent parts, one for each index of `dp`. The reference program is written for one: setup_inputs(seed, part) draws one part's arguments, and reference() takes and returns one part's arrays. A program takes and returns all parts, laid end to end along the dimension named above; an argument that names none is the same for every part. Nothing has to cross between parts.
Inputs may be any that keep to these rules, and one draw needn't show every extreme that they name: `expert_ids`: each token names 8 different experts. `slot_ids`: within one micro-batch, one block of 48 tokens and one expert, the assignments are numbered 0, 1, 2, ... in a drawn priority order; an assignment keeps its number as slot if it is below 8, else it is -1. In every block some expert receives an assignment from each of its 48 tokens.
All inputs are finite; a program needn't handle non-finite values.
Results may differ from the reference program's by a relative error of at most 0.0057.
Values may be sent and summed in bfloat16 or wider, within the bound.
A program may use at most 64 MiB of HBM per device.

```python
import jax
import jax.numpy as jnp
from jax import lax

D = 2048
HID = 1024
TOP = 8
MICRO = 2
TOK_DEV = 48
EXPERTS = 64
TOKENS = 3072
SLOTS = 8


def routing_draw(key):
    key_bias, key_noise, key_hot, key_order = jax.random.split(key, 4)
    hot_expert = jax.random.randint(key_hot, (), 0, EXPERTS)
    expert_bias = jax.random.randint(key_bias, (EXPERTS,), 0, 1 << 14)
    token_noise = jax.random.randint(key_noise, (MICRO, TOKENS, EXPERTS), 0, 1 << 14)
    column = jnp.arange(EXPERTS, dtype=jnp.int32)
    scores = (token_noise + expert_bias[None, None, :] + jnp.where(column == hot_expert, 1 << 16, 0)[None, None, :]) * EXPERTS + column[None, None, :]
    chosen = lax.top_k(scores, TOP)[1].astype(jnp.int32)
    length = TOK_DEV * TOP
    blocks = TOKENS // TOK_DEV
    flat_chosen = chosen.reshape(MICRO, blocks, length)
    position = jnp.arange(length, dtype=jnp.int32)
    priority = jax.random.randint(key_order, (MICRO, blocks, length), 0, 1 << 12) * length + position[None, None, :]
    same = flat_chosen[..., :, None] == flat_chosen[..., None, :]
    before = priority[..., None, :] < priority[..., :, None]
    number = jnp.sum((same & before).astype(jnp.int32), axis=-1).reshape(MICRO, TOKENS, TOP)
    places = jnp.where(number < SLOTS, number, -1).astype(jnp.int32)
    return (chosen, places)


def draw_expert_ids(key, part):
    return routing_draw(key)[0]


def draw_slot_ids(key, part):
    return routing_draw(key)[1]


def shard_levels(key, dims, pieces, low, high):
    gain = 1.0
    for dim, parts in pieces:
        heights = jax.random.uniform(jax.random.fold_in(jax.random.fold_in(key, 6), dim), (parts,), jnp.float32, low / len(pieces), high / len(pieces))
        gain = gain * jnp.repeat(jnp.exp(heights), dims[dim] // parts).reshape((-1,) + (1,) * (len(dims) - 1 - dim))
    return gain


def centred(stream_key, dims, deviation, reach, shards=(), held_as=jnp.bfloat16):
    gain = shard_levels(stream_key, dims, shards, -0.22, 0.18) if shards else 1.0
    result = jax.random.normal(stream_key, dims, jnp.float32) * deviation * gain
    return jnp.minimum(jnp.maximum(result, -reach), reach).astype(held_as)


def setup_inputs(seed: int = 0, part: int = 0) -> dict:
    splits = jax.random.split(jax.random.key(seed), 8)
    part_splits = jax.random.split(jax.random.fold_in(splits[7], part), 8)
    tokens = centred(part_splits[0], (MICRO, TOKENS, D), 1.0, 6.0, ((1, 64),))
    expert_ids = draw_expert_ids(jax.random.fold_in(jax.random.fold_in(splits[7], part), 71), part)
    slot_ids = draw_slot_ids(jax.random.fold_in(jax.random.fold_in(splits[7], part), 71), part)
    gate_values = jnp.clip(0.05 + 0.95 * jax.random.uniform(part_splits[3], (MICRO, TOKENS, TOP), jnp.float32) ** shard_levels(part_splits[3], (MICRO, TOKENS, TOP), ((1, 64),), -0.2, 0.2), 0.05, 1.0)
    gate_weight = centred(splits[4], (EXPERTS, D, HID), D ** -0.5, 0.125, ((0, 64),))
    up_weight = centred(splits[5], (EXPERTS, D, HID), D ** -0.5, 0.125, ((0, 64),))
    down_weight = centred(splits[6], (EXPERTS, HID, D), HID ** -0.5, 0.1875, ((0, 64),))
    return {"tokens": tokens, "expert_ids": expert_ids, "slot_ids": slot_ids, "gate_values": gate_values, "gate_weight": gate_weight, "up_weight": up_weight, "down_weight": down_weight}


def expert_block(packed):
    rows, gate_matrix, up_matrix, down_matrix = packed
    flat = rows.reshape(-1, D)
    gate_part = jnp.dot(flat, gate_matrix, preferred_element_type=jnp.float32)
    up_part = jnp.dot(flat, up_matrix, preferred_element_type=jnp.float32)
    hidden = (jax.nn.silu(gate_part) * up_part).astype(jnp.bfloat16)
    output = jnp.dot(hidden, down_matrix, preferred_element_type=jnp.float32).astype(jnp.bfloat16)
    return output.reshape(rows.shape)


def reference(tokens, expert_ids, slot_ids, gate_values, gate_weight, up_weight, down_weight):
    sources = TOKENS // TOK_DEV
    source = jnp.broadcast_to((jnp.arange(TOKENS, dtype=jnp.int32) // TOK_DEV)[:, None], (TOKENS, TOP))
    results = []
    for index in range(MICRO):
        chosen = expert_ids[index]
        places = slot_ids[index]
        kept_mask = places >= 0
        slot_place = jnp.where(kept_mask, places, SLOTS).astype(jnp.int32)
        copies = jnp.broadcast_to(tokens[index][:, None, :], (TOKENS, TOP, D))
        buffer = jnp.zeros((EXPERTS, sources, SLOTS, D), jnp.bfloat16)
        buffer = buffer.at[chosen, source, slot_place].set(copies, mode="drop")
        answers = lax.map(expert_block, (buffer, gate_weight, up_weight, down_weight))
        picked = answers[chosen, source, jnp.where(kept_mask, places, 0).astype(jnp.int32)]
        weighting = jnp.where(kept_mask, gate_values[index], jnp.float32(0.0)).astype(jnp.float32)
        mixture = jnp.einsum("tk,tkd->td", weighting, picked.astype(jnp.float32), precision=lax.Precision.HIGHEST)
        results.append(mixture.astype(jnp.bfloat16))
    return jnp.stack(results, axis=0)
```

```python
import functools

import jax
import jax.numpy as jnp
from jax import lax
from jax.experimental import pallas as pl
from jax.experimental.pallas import tpu as pltpu
from jax.sharding import PartitionSpec as P

MESH = pl.DeviceIdType.MESH
RING = 8
GROUP = 8
SLOTS = 8
ROWS = 2 * SLOTS
PAIR = GROUP * ROWS
PAIRS = RING // 2
UP, DOWN = 0, 1


def kernel(
    ids_ref, places_ref, gates_ref, tokens_ref, gate_ref, up_ref, down_ref, out_ref,
    wg, wu, wd, blocks, meta, turn, snd, rcv, hidden, answers, ret, acc, rs_out, rs_in, result,
    weight_sem, tok_sem, out_sem,
    meta_send, meta_recv, ag_send, ag_recv, d_send, d_recv, r_send, r_recv, rs_send, rs_recv,
):
    micro, tok, width = tokens_ref.shape
    half = width // 2
    chunks = [slice(0, half), slice(half, width)]
    ex, ey = lax.axis_index("ex"), lax.axis_index("ey")
    z = ex // 2
    me = lax.rem(ex, 2) * 4 + ey

    def along(step):
        return {"ex": lax.rem(z + step + RING, RING) * 2 + lax.rem(ex, 2), "ey": ey}

    def partner(step):
        other = lax.rem(me + step + GROUP, GROUP)
        return {"ex": z * 2 + other // 4, "ey": lax.rem(other, 4)}

    def remote(src, dst, send, recv, device):
        return pltpu.make_async_remote_copy(
            src_ref=src, dst_ref=dst, send_sem=send, recv_sem=recv,
            device_id=device, device_id_type=MESH,
        )

    tok_copies = [
        pltpu.make_async_copy(tokens_ref.at[m], blocks.at[m, 0, pl.ds(0, tok)], tok_sem.at[m])
        for m in range(micro)
    ]
    for copy in tok_copies:
        copy.start()
    weight_copies = [
        pltpu.make_async_copy(src.at[0], dst, weight_sem.at[i])
        for i, (src, dst) in enumerate(((gate_ref, wg), (up_ref, wu), (down_ref, wd)))
    ]
    for copy in weight_copies:
        copy.start()

    barrier = pltpu.get_barrier_semaphore()
    for device in [along(1), along(-1)] + [partner(r) for r in range(1, GROUP)]:
        pl.semaphore_signal(barrier, inc=1, device_id=device, device_id_type=MESH)

    turn[...] = jnp.zeros_like(turn)
    for m in range(micro):
        code = jnp.where(places_ref[m] >= 0, ids_ref[m] * SLOTS + places_ref[m], -1)
        turn[0, 0:tok, 0:8] = code.astype(jnp.float32)
        turn[1, 0:tok, 0:8] = gates_ref[m]
        meta[0, 0, m, 0:8, :] = turn[0].T[0:8]
        meta[0, 0, m, 8:16, :] = turn[1].T[0:8]

    pl.semaphore_wait(barrier, GROUP + 1)

    sent = []

    def block(m, d, way, c):
        pair, part = (d, way) if 0 < d < PAIRS else ((0, 0) if d == 0 else (0, 1))
        return blocks.at[m, pair, pl.ds(part * tok, tok), chunks[c]]

    def pass_block(m, d, way, c):
        if d == PAIRS - 1 and c != way:
            return
        copy = remote(
            block(m, d, way, c), block(m, d + 1, way, c),
            ag_send.at[m, way, d, c], ag_recv.at[m, way, d, c], along(1 if way == UP else -1),
        )
        copy.start()
        sent.append(copy)

    def await_block(m, d, way, c):
        if d == PAIRS and c != way:
            return
        remote(
            block(m, d - 1, way, c), block(m, d, way, c),
            ag_send.at[m, way, d - 1, c], ag_recv.at[m, way, d - 1, c], along(0),
        ).wait_recv()

    def meta_at(d, way):
        pair, part = (d, way) if 0 < d < PAIRS else ((0, 0) if d == 0 else (0, 1))
        return meta.at[pair, part]

    def pass_meta(d, way):
        if d == PAIRS - 1 and way != UP:
            return
        copy = remote(
            meta_at(d, way), meta_at(d + 1, way), meta_send.at[way, d], meta_recv.at[way, d],
            along(1 if way == UP else -1),
        )
        copy.start()
        sent.append(copy)

    def await_meta(d, way):
        if d == PAIRS and way != UP:
            return
        remote(
            meta_at(d - 1, way), meta_at(d, way), meta_send.at[way, d - 1], meta_recv.at[way, d - 1], along(0)
        ).wait_recv()

    lane = lax.broadcasted_iota(jnp.int32, (8, 128), 1)
    row = lax.broadcasted_iota(jnp.int32, (PAIR, 128), 0)

    def cells(m, pair):
        places = []
        for part in range(2):
            code = meta[pair, part, m, 0:8, :].astype(jnp.int32)
            expert = code // SLOTS - z * GROUP
            turned = lax.rem(expert - me + GROUP, GROUP)
            place = turned * ROWS + part * SLOTS + lax.rem(code, SLOTS)
            good = (code >= 0) & (expert >= 0) & (expert < GROUP) & (lane < tok)
            places.append(jnp.where(good, place, -1))
        return jnp.where(lane < tok, places[0], pltpu.roll(places[1], tok, 1))

    def select(m, pair):
        where = cells(m, pair)
        hit = row == where[0:1, :]
        for k in range(1, 8):
            hit = hit | (row == where[k : k + 1, :])
        return jnp.where(hit, 1.0, 0.0).astype(jnp.bfloat16)[:, 0 : 2 * tok]

    def mixing(m, pair):
        where = cells(m, pair)
        first, second = meta[pair, 0, m, 8:16, :], meta[pair, 1, m, 8:16, :]
        gates = jnp.where(lane < tok, first, pltpu.roll(second, tok, 1))
        total = jnp.zeros((PAIR, 128), jnp.float32)
        for k in range(8):
            total = total + jnp.where(row == where[k : k + 1, :], gates[k : k + 1, :], 0.0)
        total = total.T[0 : 2 * tok]
        high = total.astype(jnp.bfloat16)
        low = (total - high.astype(jnp.float32)).astype(jnp.bfloat16)
        return high, low

    def spread(m, pair, c, source, target, send, recv, back):
        for r in range(1, GROUP):
            at = pl.ds(pair * PAIR + r * ROWS, ROWS)
            copy = remote(
                source.at[m, at, chunks[c]], target.at[m, at, chunks[c]],
                send.at[m, pair, c], recv.at[m, pair, c], partner(-r if back else r),
            )
            copy.start()

    def others(buffer, m, pair, c):
        return buffer.at[m, pl.ds(pair * PAIR + ROWS, PAIR - ROWS), chunks[c]]

    def await_spread(m, pair, c, source, target, send, recv):
        remote(
            others(source, m, pair, c), others(target, m, pair, c),
            send.at[m, pair, c], recv.at[m, pair, c], along(0),
        ).wait_recv()

    def finish_spread(m, pair, c, source, target, send, recv):
        remote(
            others(source, m, pair, c), others(target, m, pair, c),
            send.at[m, pair, c], recv.at[m, pair, c], along(0),
        ).wait_send()

    def start_ring(m):
        tok_copies[m].wait()
        for c in range(2):
            for way in (UP, DOWN):
                pass_block(m, 0, way, c)

    order = [1, 2, 3, 0]
    start_ring(0)
    pass_meta(0, UP)
    pass_meta(0, DOWN)
    for m in range(micro):
        for pair in order:
            d = pair if pair else PAIRS
            for c in range(2):
                if m == 0 and c == 0:
                    for way in (UP, DOWN):
                        await_meta(d, way)
                        if d < PAIRS:
                            pass_meta(d, way)
                for way in (UP, DOWN):
                    await_block(m, d, way, c)
                    if d < PAIRS:
                        pass_block(m, d, way, c)
                if pair == 3 and c == 1 and m + 1 < micro:
                    start_ring(m + 1)
                chosen = jnp.dot(
                    select(m, pair), blocks[m, pair, :, chunks[c]], preferred_element_type=jnp.float32
                ).astype(jnp.bfloat16)
                base = pair * PAIR
                rcv[m, base : base + ROWS, chunks[c]] = chosen[0:ROWS]
                snd[m, base + ROWS : base + PAIR, chunks[c]] = chosen[ROWS:PAIR]
                spread(m, pair, c, snd, rcv, d_send, d_recv, False)

    tile = 256

    def expert(m):
        for pair in order:
            for c in range(2):
                await_spread(m, pair, c, snd, rcv, d_send, d_recv)

        @pl.loop(0, wg.shape[1] // tile)
        def _(i):
            at = pl.ds(pl.multiple_of(i * tile, tile), tile)
            gate_part = jnp.dot(rcv[m], wg[:, at], preferred_element_type=jnp.float32)
            up_part = jnp.dot(rcv[m], wu[:, at], preferred_element_type=jnp.float32)
            hidden[:, at] = (gate_part / (1.0 + jnp.exp(-gate_part)) * up_part).astype(jnp.bfloat16)

        @pl.loop(0, width // tile)
        def _(i):
            at = pl.ds(pl.multiple_of(i * tile, tile), tile)
            answer = jnp.dot(hidden[...], wd[:, at], preferred_element_type=jnp.float32)
            answers[m, :, at] = answer.astype(jnp.bfloat16)

        for pair in (0, 3, 2, 1):
            base = pair * PAIR
            for c in range(2):
                spread(m, pair, c, answers, ret, r_send, r_recv, True)
            ret[m, base : base + ROWS, :] = answers[m, base : base + ROWS, :]

    for copy in weight_copies:
        copy.wait()
    for m in range(micro):
        expert(m)

    def sum_copy(m, d, way, c):
        return remote(
            rs_out.at[m, way, d - 1, :, chunks[c]], rs_in.at[m, way, d - 1, :, chunks[c]],
            rs_send.at[m, way, d - 1, c], rs_recv.at[m, way, d - 1, c], along(-1 if way == UP else 1),
        )

    out_copies = []
    for m in range(micro):
        for pair in (0, 3, 2, 1):
            high, low = mixing(m, pair)
            base = pair * PAIR
            for c in range(2):
                await_spread(m, pair, c, answers, ret, r_send, r_recv)
                rows = ret[m, base : base + PAIR, chunks[c]]
                part = jnp.dot(high, rows, preferred_element_type=jnp.float32)
                part = part + jnp.dot(low, rows, preferred_element_type=jnp.float32)
                if pair == 0:
                    acc[m, :, chunks[c]] = part[0:tok]
                    rs_out[m, c, PAIRS - 1, :, chunks[c]] = part[tok : 2 * tok].astype(jnp.bfloat16)
                    copy = sum_copy(m, PAIRS, c, c)
                    copy.start()
                    sent.append(copy)
                    continue
                for way in (UP, DOWN):
                    mine = part[way * tok : (way + 1) * tok]
                    if pair < 3 or c == way:
                        sum_copy(m, pair + 1, way, c).wait_recv()
                        mine = mine + rs_in[m, way, pair, :, chunks[c]].astype(jnp.float32)
                    rs_out[m, way, pair - 1, :, chunks[c]] = mine.astype(jnp.bfloat16)
                    copy = sum_copy(m, pair, way, c)
                    copy.start()
                    sent.append(copy)
        for c in range(2):
            total = acc[m, :, chunks[c]]
            for way in (UP, DOWN):
                sum_copy(m, 1, way, c).wait_recv()
                total = total + rs_in[m, way, 0, :, chunks[c]].astype(jnp.float32)
            result[m, :, chunks[c]] = total.astype(jnp.bfloat16)
        copy = pltpu.make_async_copy(result.at[m], out_ref.at[m], out_sem.at[m])
        copy.start()
        out_copies.append(copy)

    for copy in sent:
        copy.wait_send()
    for m in range(micro):
        for pair in range(PAIRS):
            for c in range(2):
                finish_spread(m, pair, c, snd, rcv, d_send, d_recv)
                finish_spread(m, pair, c, answers, ret, r_send, r_recv)
    for copy in out_copies:
        copy.wait()


def per_device(tokens, expert_ids, slot_ids, gate_values, gate_weight, up_weight, down_weight):
    micro, tok, width = tokens.shape
    hid = gate_weight.shape[2]
    bf16, f32 = jnp.bfloat16, jnp.float32
    vmem = pl.BlockSpec(memory_space=pltpu.VMEM)
    anywhere = pl.BlockSpec(memory_space=pl.ANY)
    dma = pltpu.SemaphoreType.DMA
    slots = PAIRS * PAIR
    return pl.pallas_call(
        kernel,
        out_shape=jax.ShapeDtypeStruct((micro, tok, width), bf16),
        in_specs=[vmem] * 3 + [anywhere] * 4,
        out_specs=anywhere,
        scratch_shapes=[
            pltpu.VMEM((width, hid), bf16),
            pltpu.VMEM((width, hid), bf16),
            pltpu.VMEM((hid, width), bf16),
            pltpu.VMEM((micro, PAIRS, 2 * tok, width), bf16),
            pltpu.VMEM((PAIRS, 2, micro, 16, 128), f32),
            pltpu.VMEM((2, 128, 128), f32),
            pltpu.VMEM((micro, slots, width), bf16),
            pltpu.VMEM((micro, slots, width), bf16),
            pltpu.VMEM((slots, hid), bf16),
            pltpu.VMEM((micro, slots, width), bf16),
            pltpu.VMEM((micro, slots, width), bf16),
            pltpu.VMEM((micro, tok, width), f32),
            pltpu.VMEM((micro, 2, PAIRS, tok, width), bf16),
            pltpu.VMEM((micro, 2, PAIRS, tok, width), bf16),
            pltpu.VMEM((micro, tok, width), bf16),
            dma((3,)),
            dma((micro,)),
            dma((micro,)),
            dma((2, PAIRS)),
            dma((2, PAIRS)),
            dma((micro, 2, PAIRS, 2)),
            dma((micro, 2, PAIRS, 2)),
            dma((micro, PAIRS, 2)),
            dma((micro, PAIRS, 2)),
            dma((micro, PAIRS, 2)),
            dma((micro, PAIRS, 2)),
            dma((micro, 2, PAIRS, 2)),
            dma((micro, 2, PAIRS, 2)),
        ],
        compiler_params=pltpu.CompilerParams(
            collective_id=0, has_side_effects=True, vmem_limit_bytes=60 * 1024 * 1024
        ),
        cost_estimate=pl.CostEstimate(
            flops=2 * micro * slots * 3 * width * hid,
            bytes_accessed=3 * width * hid * 2,
            transcendentals=micro * slots * hid,
        ),
        name="experts",
    )(expert_ids, slot_ids, gate_values, tokens, gate_weight, up_weight, down_weight)


def solution(mesh):
    tokens = P(None, ("dp", "ex", "ey"), None)
    weights = P(("ex", "ey"), None, None)
    return jax.shard_map(
        per_device,
        mesh=mesh,
        in_specs=(tokens,) * 4 + (weights,) * 3,
        out_specs=tokens,
        check_vma=False,
    )
```

```python
import jax
import jax.numpy as jnp
from jax import lax
from jax.experimental import pallas as pl
from jax.experimental.pallas import tpu as pltpu
from jax.sharding import PartitionSpec as P

MESH = pl.DeviceIdType.MESH
RING = 8
FAR = RING // 2
GROUP = 8
SLOTS = 8
ROWS = 2 * SLOTS
STAGE = GROUP * ROWS
UP, DOWN = 0, 1

STAGES = 8
FIRST = 5
EARLY = (3,)
LATE = (7, 5, 6, 4, 1, 2, 0)


def place_of(m, d, way):
    if d == 0:
        return 0, m
    if d == FAR:
        return STAGES - 1, m
    return 2 * d - 1 + m, way


def kernel(
    ids_ref, places_ref, gates_ref, tokens_ref, gate_ref, up_ref, down_ref, out_ref,
    wg, wu, wd, ids, places, gates, blocks, meta, snd, rcv, hidden, answers, ret, rs_out, rs_in, result,
    weight_sem, tok_sem, route_sem, out_sem,
    meta_send, meta_recv, ag_send, ag_recv, d_send, d_recv, r_send, r_recv, rs_send, rs_recv,
):
    micro, tok, width = tokens_ref.shape
    half = width // 2
    chunks = [slice(0, half), slice(half, width)]
    ex, ey = lax.axis_index("ex"), lax.axis_index("ey")
    z = ex // 2
    me = lax.rem(ex, 2) * 4 + ey

    def along(step):
        return {"ex": lax.rem(z + step + RING, RING) * 2 + lax.rem(ex, 2), "ey": ey}

    def partner(step):
        other = lax.rem(me + step + GROUP, GROUP)
        return {"ex": z * 2 + other // 4, "ey": lax.rem(other, 4)}

    def remote(src, dst, send, recv, device):
        return pltpu.make_async_remote_copy(
            src_ref=src, dst_ref=dst, send_sem=send, recv_sem=recv,
            device_id=device, device_id_type=MESH,
        )

    barrier = pltpu.get_barrier_semaphore()
    for device in [along(1), along(-1)] + [partner(r) for r in range(1, GROUP)]:
        pl.semaphore_signal(barrier, inc=1, device_id=device, device_id_type=MESH)

    tok_copies = [
        pltpu.make_async_copy(tokens_ref.at[m], blocks.at[0, pl.ds(m * tok, tok)], tok_sem.at[m])
        for m in range(micro)
    ]
    route_copies = [
        pltpu.make_async_copy(src, dst, route_sem.at[i])
        for i, (src, dst) in enumerate(((ids_ref, ids), (places_ref, places), (gates_ref, gates)))
    ]
    weight_copies = [
        pltpu.make_async_copy(src.at[0], dst, weight_sem.at[i])
        for i, (src, dst) in enumerate(((gate_ref, wg), (up_ref, wu), (down_ref, wd)))
    ]
    for copy in tok_copies + route_copies + weight_copies:
        copy.start()

    meta[0] = jnp.zeros_like(meta[0])
    for copy in route_copies:
        copy.wait()
    for m in range(micro):
        code = jnp.where(places[m] >= 0, ids[m] * SLOTS + places[m], -1)
        meta[0, m, 0:8, 0:tok] = code.astype(jnp.float32)
        meta[0, m, 8:16, 0:tok] = gates[m]
    for copy in tok_copies:
        copy.wait()
    pl.semaphore_wait(barrier, GROUP + 1)

    sent = []

    def block(m, d, way, c):
        stage, part = place_of(m, d, way)
        return blocks.at[stage, pl.ds(part * tok, tok), chunks[c]]

    def block_copy(m, d, way, c):
        return remote(
            block(m, d, way, c), block(m, d + 1, way, c),
            ag_send.at[m, way, d, c], ag_recv.at[m, way, d, c], along(1 if way == UP else -1),
        )

    def meta_copy(m, d, way):
        return remote(
            meta.at[place_of(m, d, way)], meta.at[place_of(m, d + 1, way)],
            meta_send.at[m, way, d], meta_recv.at[m, way, d], along(1 if way == UP else -1),
        )

    def pass_block(m, d, way, c):
        if d < FAR - 1 or c == way:
            copy = block_copy(m, d, way, c)
            copy.start()
            sent.append(copy)

    def pass_meta(m, d, way):
        if d < FAR - 1 or way == UP:
            copy = meta_copy(m, d, way)
            copy.start()
            sent.append(copy)

    lane = lax.broadcasted_iota(jnp.int32, (8, 128), 1)
    row = lax.broadcasted_iota(jnp.int32, (STAGE, 128), 0)

    def cells(stage):
        found = []
        for part in range(2):
            code = meta[stage, part, 0:8, :].astype(jnp.int32)
            expert = code // SLOTS - z * GROUP
            turned = lax.rem(expert - me + GROUP, GROUP)
            place = turned * ROWS + part * SLOTS + lax.rem(code, SLOTS)
            good = (code >= 0) & (expert >= 0) & (expert < GROUP) & (lane < tok)
            found.append(jnp.where(good, place, -1))
        return jnp.where(lane < tok, found[0], pltpu.roll(found[1], tok, 1))

    def select(stage):
        where = cells(stage)
        hit = row == where[0:1, :]
        for k in range(1, 8):
            hit = hit | (row == where[k : k + 1, :])
        return jnp.where(hit, 1.0, 0.0).astype(jnp.bfloat16)[:, 0 : 2 * tok]

    def mixing(stage):
        where = cells(stage)
        first, second = meta[stage, 0, 8:16, :], meta[stage, 1, 8:16, :]
        weight = jnp.where(lane < tok, first, pltpu.roll(second, tok, 1))
        total = jnp.zeros((STAGE, 128), jnp.float32)
        for k in range(8):
            total = total + jnp.where(row == where[k : k + 1, :], weight[k : k + 1, :], 0.0)
        total = total.T[0 : 2 * tok]
        high = total.astype(jnp.bfloat16)
        low = (total - high.astype(jnp.float32)).astype(jnp.bfloat16)
        return high, low

    def spread(stage, c, source, target, send, recv, back):
        for r in range(1, GROUP):
            at = pl.ds(stage * STAGE + r * ROWS, ROWS)
            remote(
                source.at[at, chunks[c]], target.at[at, chunks[c]],
                send.at[stage, c], recv.at[stage, c], partner(-r if back else r),
            ).start()

    def whole_spread(stage, c, source, target, send, recv):
        at = pl.ds(stage * STAGE + ROWS, STAGE - ROWS)
        return remote(
            source.at[at, chunks[c]], target.at[at, chunks[c]], send.at[stage, c], recv.at[stage, c], along(0)
        )

    for m in range(micro):
        for c in range(2):
            for way in (UP, DOWN):
                pass_block(m, 0, way, c)
                if c == 0:
                    pass_meta(m, 0, way)
    for stage in range(STAGES):
        for c in range(2):
            if 0 < stage < STAGES - 1:
                d, m = (stage + 1) // 2, (stage + 1) % 2
                for way in (UP, DOWN):
                    block_copy(m, d - 1, way, c).wait_recv()
                    pass_block(m, d, way, c)
                    if c == 0:
                        meta_copy(m, d - 1, way).wait_recv()
                        pass_meta(m, d, way)
            elif stage:
                for m in range(micro):
                    block_copy(m, FAR - 1, c, c).wait_recv()
                    if c == 0:
                        meta_copy(m, FAR - 1, UP).wait_recv()
            if c == 0:
                choice = select(stage)
            chosen = jnp.dot(
                choice, blocks[stage, :, chunks[c]], preferred_element_type=jnp.float32
            ).astype(jnp.bfloat16)
            base = stage * STAGE
            rcv[base : base + ROWS, chunks[c]] = chosen[0:ROWS]
            snd[base + ROWS : base + STAGE, chunks[c]] = chosen[ROWS:STAGE]
            spread(stage, c, snd, rcv, d_send, d_recv, False)

    tile = 256

    def expert(first, last):
        at_rows = slice(first * STAGE, last * STAGE)
        for stage in range(first, last):
            for c in range(2):
                whole_spread(stage, c, snd, rcv, d_send, d_recv).wait_recv()

        @pl.loop(0, wg.shape[1] // tile)
        def _(i):
            at = pl.ds(pl.multiple_of(i * tile, tile), tile)
            gate_part = jnp.dot(rcv[at_rows], wg[:, at], preferred_element_type=jnp.float32)
            up_part = jnp.dot(rcv[at_rows], wu[:, at], preferred_element_type=jnp.float32)
            hidden[at_rows, at] = (gate_part / (1.0 + jnp.exp(-gate_part)) * up_part).astype(jnp.bfloat16)

        @pl.loop(0, width // tile)
        def _(i):
            at = pl.ds(pl.multiple_of(i * tile, tile), tile)
            answer = jnp.dot(hidden[at_rows], wd[:, at], preferred_element_type=jnp.float32)
            answers[at_rows, at] = answer.astype(jnp.bfloat16)

    def give_back(stage):
        base = stage * STAGE
        for c in range(2):
            spread(stage, c, answers, ret, r_send, r_recv, True)
        ret[base : base + ROWS, :] = answers[base : base + ROWS, :]

    for copy in weight_copies:
        copy.wait()
    expert(0, FIRST)
    for stage in EARLY:
        give_back(stage)
    expert(FIRST, STAGES)
    for stage in LATE:
        give_back(stage)

    def sum_copy(m, d, way, c):
        return remote(
            rs_out.at[m, way, d - 1, :, chunks[c]], rs_in.at[m, way, d - 1, :, chunks[c]],
            rs_send.at[m, way, d - 1, c], rs_recv.at[m, way, d - 1, c], along(-1 if way == UP else 1),
        )

    def send_sum(m, d, way, c, value):
        rs_out[m, way, d - 1, :, chunks[c]] = value.astype(jnp.bfloat16)
        copy = sum_copy(m, d, way, c)
        copy.start()
        sent.append(copy)

    for stage in reversed(range(STAGES)):
        high, low = mixing(stage)
        base = stage * STAGE
        for c in range(2):
            whole_spread(stage, c, answers, ret, r_send, r_recv).wait_recv()
            rows = ret[base : base + STAGE, chunks[c]]
            part = jnp.dot(high, rows, preferred_element_type=jnp.float32)
            part = part + jnp.dot(low, rows, preferred_element_type=jnp.float32)
            for j in range(2):
                mine = part[j * tok : (j + 1) * tok]
                if stage == STAGES - 1:
                    send_sum(j, FAR, c, c, mine)
                elif stage:
                    d, m = (stage + 1) // 2, (stage + 1) % 2
                    if d < FAR - 1 or c == j:
                        sum_copy(m, d + 1, j, c).wait_recv()
                        mine = mine + rs_in[m, j, d, :, chunks[c]].astype(jnp.float32)
                    send_sum(m, d, j, c, mine)
                else:
                    for way in (UP, DOWN):
                        sum_copy(j, 1, way, c).wait_recv()
                        mine = mine + rs_in[j, way, 0, :, chunks[c]].astype(jnp.float32)
                    result[j, :, chunks[c]] = mine.astype(jnp.bfloat16)
    out_copy = pltpu.make_async_copy(result, out_ref, out_sem)
    out_copy.start()

    for copy in sent:
        copy.wait_send()
    for stage in range(STAGES):
        for c in range(2):
            whole_spread(stage, c, snd, rcv, d_send, d_recv).wait_send()
            whole_spread(stage, c, answers, ret, r_send, r_recv).wait_send()
    out_copy.wait()


def per_device(tokens, expert_ids, slot_ids, gate_values, gate_weight, up_weight, down_weight):
    micro, tok, width = tokens.shape
    hid = gate_weight.shape[2]
    bf16, f32, i32 = jnp.bfloat16, jnp.float32, jnp.int32
    anywhere = pl.BlockSpec(memory_space=pl.ANY)
    dma = pltpu.SemaphoreType.DMA
    slots = STAGES * STAGE
    routes = [a.swapaxes(1, 2) for a in (expert_ids, slot_ids, gate_values)]
    return pl.pallas_call(
        kernel,
        out_shape=jax.ShapeDtypeStruct((micro, tok, width), bf16),
        in_specs=[anywhere] * 7,
        out_specs=anywhere,
        scratch_shapes=[
            pltpu.VMEM((width, hid), bf16),
            pltpu.VMEM((width, hid), bf16),
            pltpu.VMEM((hid, width), bf16),
            pltpu.VMEM((micro, 8, tok), i32),
            pltpu.VMEM((micro, 8, tok), i32),
            pltpu.VMEM((micro, 8, tok), f32),
            pltpu.VMEM((STAGES, 2 * tok, width), bf16),
            pltpu.VMEM((STAGES, 2, 16, 128), f32),
            pltpu.VMEM((slots, width), bf16),
            pltpu.VMEM((slots, width), bf16),
            pltpu.VMEM((slots, hid), bf16),
            pltpu.VMEM((slots, width), bf16),
            pltpu.VMEM((slots, width), bf16),
            pltpu.VMEM((micro, 2, FAR, tok, width), bf16),
            pltpu.VMEM((micro, 2, FAR, tok, width), bf16),
            pltpu.VMEM((micro, tok, width), bf16),
            dma((3,)),
            dma((micro,)),
            dma((3,)),
            dma,
            dma((micro, 2, FAR)),
            dma((micro, 2, FAR)),
            dma((micro, 2, FAR, 2)),
            dma((micro, 2, FAR, 2)),
            dma((STAGES, 2)),
            dma((STAGES, 2)),
            dma((STAGES, 2)),
            dma((STAGES, 2)),
            dma((micro, 2, FAR, 2)),
            dma((micro, 2, FAR, 2)),
        ],
        compiler_params=pltpu.CompilerParams(
            collective_id=0, has_side_effects=True, vmem_limit_bytes=60 * 1024 * 1024
        ),
        cost_estimate=pl.CostEstimate(
            flops=2 * slots * 3 * width * hid,
            bytes_accessed=3 * width * hid * 2,
            transcendentals=slots * hid,
        ),
        name="experts",
    )(*routes, tokens, gate_weight, up_weight, down_weight)


def solution(mesh):
    tokens = P(None, ("dp", "ex", "ey"), None)
    weights = P(("ex", "ey"), None, None)
    return jax.shard_map(
        per_device,
        mesh=mesh,
        in_specs=(tokens,) * 4 + (weights,) * 3,
        out_specs=tokens,
        check_vma=False,
    )
```

```python
import jax
import jax.numpy as jnp
from jax import lax
from jax.experimental import pallas as pl
from jax.experimental.pallas import tpu as pltpu
from jax.sharding import PartitionSpec as P

MESH = pl.DeviceIdType.MESH
RING = 8
FAR = RING // 2
GROUP = 8
SLOTS = 8
ROWS = 2 * SLOTS
STAGE = GROUP * ROWS
UP, DOWN = 0, 1

STAGES = 8
STEPS = (0, 1, 7, 2, 6, 3, 5, 4)
FIRST = 5
EARLY = (3,)
LATE = (7, 5, 6, 4, 1, 2, 0)
SIDE = 256
ACROSS = GROUP // 2


def stage_of(d, way):
    return 0 if d == 0 else STAGES - 1 if d == FAR else 2 * d - 1 + way


def kernel(
    ids_ref, places_ref, gates_ref, tokens_ref, gate_ref, up_ref, down_ref, out_ref,
    wg, wu, wd, ids, places, gates, blocks, meta, snd, rcv, hidden, answers, ret, rs_out, rs_in, result,
    side_blocks, side_meta, side_snd, side_ret, side_out, side_in, side_own,
    weight_sem, tok_sem, route_sem, out_sem,
    meta_send, meta_recv, ag_send, ag_recv, d_send, d_recv, r_send, r_recv, rs_send, rs_recv,
    sb_send, sb_recv, sm_send, sm_recv, sd_send, sd_recv, sr_send, sr_recv, sx_send, sx_recv,
):
    micro, tok, width = tokens_ref.shape
    pair = micro * tok
    half = (width - SIDE) // 2
    chunks = [slice(SIDE, SIDE + half), slice(SIDE + half, width)]
    side = slice(0, SIDE)
    ex, ey = lax.axis_index("ex"), lax.axis_index("ey")
    z = ex // 2
    y = lax.rem(ex, 2) * 2 + ey // 2
    core = lax.rem(ey, 2)

    def device(dz, dy, dc):
        there_z = lax.rem(z + dz + RING, RING)
        there_y = lax.rem(y + dy + ACROSS, ACROSS)
        there_core = lax.rem(core + dc, 2)
        return {"ex": there_z * 2 + there_y // 2, "ey": lax.rem(there_y, 2) * 2 + there_core}

    def partner(r, back=False):
        return device(0, -(r // 2) if back else r // 2, r % 2)

    def remote(src, dst, send, recv, there):
        return pltpu.make_async_remote_copy(
            src_ref=src, dst_ref=dst, send_sem=send, recv_sem=recv, device_id=there, device_id_type=MESH
        )

    met = [partner(r) for r in range(1, GROUP)] + [device(1, 0, 0), device(-1, 0, 0)]
    barrier = pltpu.get_barrier_semaphore()
    for there in met:
        pl.semaphore_signal(barrier, inc=1, device_id=there, device_id_type=MESH)

    tok_copies = [
        pltpu.make_async_copy(tokens_ref.at[m], blocks.at[0, pl.ds(m * tok, tok)], tok_sem.at[m])
        for m in range(micro)
    ]
    route_copies = [
        pltpu.make_async_copy(src, dst, route_sem.at[i])
        for i, (src, dst) in enumerate(((ids_ref, ids), (places_ref, places), (gates_ref, gates)))
    ]
    weight_copies = [
        pltpu.make_async_copy(src.at[0], dst, weight_sem.at[i])
        for i, (src, dst) in enumerate(((gate_ref, wg), (up_ref, wu), (down_ref, wd)))
    ]
    for copy in tok_copies + route_copies + weight_copies:
        copy.start()

    meta[0] = jnp.zeros_like(meta[0])
    for copy in route_copies:
        copy.wait()
    for m in range(micro):
        code = jnp.where(places[m] >= 0, ids[m] * SLOTS + places[m], -1)
        meta[0, m, 0:8, 0:tok] = code.astype(jnp.float32)
        meta[0, m, 8:16, 0:tok] = gates[m]
    for copy in tok_copies:
        copy.wait()
    pl.semaphore_wait(barrier, len(met))

    sent = []

    def start(copy):
        copy.start()
        sent.append(copy)

    def block_copy(d, way, m, c):
        at = pl.ds(m * tok, tok)
        return remote(
            blocks.at[stage_of(d, way), at, chunks[c]], blocks.at[stage_of(d + 1, way), at, chunks[c]],
            ag_send.at[way, d, m, c], ag_recv.at[way, d, m, c], device(1 if way == UP else -1, 0, 0),
        )

    def meta_copy(d, way):
        return remote(
            meta.at[stage_of(d, way)], meta.at[stage_of(d + 1, way)],
            meta_send.at[way, d], meta_recv.at[way, d], device(1 if way == UP else -1, 0, 0),
        )

    def pass_block(d, way, m, c):
        if d < FAR - 1 or c == way:
            start(block_copy(d, way, m, c))

    def pass_meta(d, way):
        if d < FAR - 1 or way == UP:
            start(meta_copy(d, way))

    lane = lax.broadcasted_iota(jnp.int32, (8, 128), 1)

    def joined(both):
        return jnp.where(lane < tok, both[0], pltpu.roll(both[1], tok, 1))

    def cells(info, mode):
        found = []
        for m in range(micro):
            code = info[m, 0:8, :].astype(jnp.int32)
            expert = code // SLOTS
            far, near = expert // GROUP, lax.rem(expert, GROUP)
            turn = lax.rem(near // 2 - y + ACROSS, ACROSS)
            other = lax.rem(near + core, 2)
            if mode == "side":
                u = lax.rem(far - z + RING, RING)
                stage = jnp.where(u == 0, 0, jnp.where(u < FAR, 2 * u - 1, jnp.where(u == FAR, 7, 2 * (RING - u))))
                good = turn == 0
                at = stage * 2 + other
            else:
                good = far == z
                at = turn * 2 + other
            at = at * ROWS + m * SLOTS + lax.rem(code, SLOTS)
            found.append(jnp.where((code >= 0) & good & (lane < tok), at, -1))
        return joined(found)

    def select(info, mode, rows):
        where = cells(info, mode)
        row = lax.broadcasted_iota(jnp.int32, (rows, 128), 0)
        hit = row == where[0:1, :]
        for k in range(1, 8):
            hit = hit | (row == where[k : k + 1, :])
        return jnp.where(hit, 1.0, 0.0).astype(jnp.bfloat16)[:, 0:pair]

    def mixing(info, mode, rows):
        where = cells(info, mode)
        weight = joined([info[m, 8:16, :] for m in range(micro)])
        row = lax.broadcasted_iota(jnp.int32, (rows, 128), 0)
        total = jnp.zeros((rows, 128), jnp.float32)
        for k in range(8):
            total = total + jnp.where(row == where[k : k + 1, :], weight[k : k + 1, :], 0.0)
        total = total.T[0:pair]
        high = total.astype(jnp.bfloat16)
        low = (total - high.astype(jnp.float32)).astype(jnp.bfloat16)
        return high, low

    def mix(weights, rows):
        high, low = weights
        return jnp.dot(high, rows, preferred_element_type=jnp.float32) + jnp.dot(
            low, rows, preferred_element_type=jnp.float32
        )

    def rows_of(stage, r):
        return pl.ds(stage * STAGE + r * ROWS, ROWS)

    def all_rows(stage):
        return pl.ds(stage * STAGE + ROWS, STAGE - ROWS)

    def dispatched(stage, c):
        there = snd.at[all_rows(stage), chunks[c]]
        return remote(there, there, d_send.at[stage, c], d_recv.at[stage, c], device(0, 0, 0))

    def returned(stage, c):
        there = ret.at[all_rows(stage), chunks[c]]
        return remote(there, there, r_send.at[stage, c], r_recv.at[stage, c], device(0, 0, 0))

    def side_dispatch(stage, q):
        return remote(
            side_snd.at[stage, q], rcv.at[stage, :, q, :, side],
            sd_send.at[stage, q], sd_recv.at[stage, q], device(STEPS[stage], 0, q),
        )

    def side_return(stage, q):
        return remote(
            answers.at[stage, :, q, :, side], side_ret.at[stage, q],
            sr_send.at[stage, q], sr_recv.at[stage, q], device(-STEPS[stage], 0, q),
        )

    side_block_copies, side_meta_copies = {}, {}
    for t in range(1, ACROSS):
        side_block_copies[t] = remote(
            blocks.at[0, :, side], side_blocks.at[t], sb_send.at[t], sb_recv.at[t], device(0, t, 0)
        )
        side_meta_copies[t] = remote(meta.at[0], side_meta.at[t], sm_send.at[t], sm_recv.at[t], device(0, t, 0))

    def side_info(t):
        return side_meta.at[t] if t else meta.at[0]

    for way in (UP, DOWN):
        pass_block(0, way, 0, 0)
        pass_meta(0, way)
    for m, c in ((1, 0), (0, 1), (1, 1)):
        for way in (UP, DOWN):
            pass_block(0, way, m, c)
    for t in (1, 3, 2):
        start(side_meta_copies[t])
        start(side_block_copies[t])

    def dispatch(stage, c, choice):
        chosen = jnp.dot(
            choice, blocks[stage, :, chunks[c]], preferred_element_type=jnp.float32
        ).astype(jnp.bfloat16)
        base = stage * STAGE
        rcv[stage, 0, 0, :, chunks[c]] = chosen[0:ROWS]
        snd[base + ROWS : base + STAGE, chunks[c]] = chosen[ROWS:STAGE]
        for r in range(1, GROUP):
            remote(
                snd.at[rows_of(stage, r), chunks[c]], rcv.at[stage, r // 2, r % 2, :, chunks[c]],
                d_send.at[stage, c], d_recv.at[stage, c], partner(r),
            ).start()

    def choose_side():
        for t in (0, 1, 3, 2):
            if t:
                side_meta_copies[t].wait_recv()
                side_block_copies[t].wait_recv()
            choice = select(side_info(t), "side", 2 * STAGE)
            tokens = side_blocks[t] if t else blocks[0, :, side]
            chosen = jnp.dot(choice, tokens, preferred_element_type=jnp.float32).astype(jnp.bfloat16)
            side_snd[:, :, t] = chosen.reshape(STAGES, 2, ROWS, SIDE)
        rcv[0, :, 0, :, side] = side_snd[0, 0]

    def dispatch_side(*stages):
        for stage in stages:
            for q in range(2):
                if (stage, q) != (0, 0):
                    start(side_dispatch(stage, q))

    def ways(d):
        return (UP, DOWN) if 0 < d < FAR else (UP,)

    def dispatch_step(d):
        choices = {}
        for c in range(2):
            for m in range(micro):
                for way in ways(d):
                    if d == FAR:
                        block_copy(d - 1, c, m, c).wait_recv()
                    elif d:
                        block_copy(d - 1, way, m, c).wait_recv()
                        pass_block(d, way, m, c)
                    if d and (m, c) == (0, 0):
                        meta_copy(d - 1, way).wait_recv()
                        if d < FAR:
                            pass_meta(d, way)
            for way in ways(d):
                stage = stage_of(d, way)
                if c == 0:
                    choices[way] = select(meta.at[stage], "ring", STAGE)
                dispatch(stage, c, choices[way])

    tile = 256

    def await_rows(first, last):
        for stage in range(first, last):
            for c in range(2):
                dispatched(stage, c).wait_recv()
            for q in range(2):
                if (stage, q) != (0, 0):
                    side_dispatch(stage, q).wait_recv()

    def expert_up(first, last):
        @pl.loop(0, wg.shape[1] // tile)
        def _(i):
            at = pl.ds(pl.multiple_of(i * tile, tile), tile)
            rows = rcv[first:last].reshape((last - first) * STAGE, width)
            gate_part = jnp.dot(rows, wg[:, at], preferred_element_type=jnp.float32)
            up_part = jnp.dot(rows, wu[:, at], preferred_element_type=jnp.float32)
            hidden[first * STAGE : last * STAGE, at] = (
                gate_part / (1.0 + jnp.exp(-gate_part)) * up_part
            ).astype(jnp.bfloat16)

    def expert_down(first, last):
        @pl.loop(0, width // tile)
        def _(i):
            at = pl.ds(pl.multiple_of(i * tile, tile), tile)
            answer = jnp.dot(
                hidden[first * STAGE : last * STAGE], wd[:, at], preferred_element_type=jnp.float32
            )
            answers[first:last, :, :, :, at] = answer.astype(jnp.bfloat16).reshape(
                last - first, ACROSS, 2, ROWS, tile
            )

    def give_back(stage):
        for c in range(2):
            for r in range(1, GROUP):
                remote(
                    answers.at[stage, r // 2, r % 2, :, chunks[c]], ret.at[rows_of(stage, r), chunks[c]],
                    r_send.at[stage, c], r_recv.at[stage, c], partner(r, True),
                ).start()
        ret[stage * STAGE : stage * STAGE + ROWS, :] = answers[stage, 0, 0]

    def give_back_side(stage):
        for q in range(2):
            if (stage, q) == (0, 0):
                side_ret[0, 0] = answers[0, :, 0, :, side]
            else:
                start(side_return(stage, q))

    dispatch_step(0)
    dispatch_step(1)
    dispatch_step(2)
    choose_side()
    dispatch_side(1, 2, 3, 4, 0)
    dispatch_step(3)
    dispatch_side(5, 6)
    for copy in weight_copies:
        copy.wait()
    await_rows(0, FIRST)
    expert_up(0, FIRST)
    dispatch_step(FAR)
    dispatch_side(7)
    expert_down(0, FIRST)
    for stage in EARLY:
        give_back(stage)
    for stage in range(FIRST):
        give_back_side(stage)
    await_rows(FIRST, STAGES)
    expert_up(FIRST, STAGES)
    expert_down(FIRST, STAGES)
    for stage in LATE:
        give_back(stage)
        if stage == STAGES - 1:
            for other in range(FIRST, STAGES):
                give_back_side(other)

    def sum_copy(d, way, m, c):
        at = pl.ds(m * tok, tok)
        return remote(
            rs_out.at[way, d - 1, at, chunks[c]], rs_in.at[way, d - 1, at, chunks[c]],
            rs_send.at[way, d - 1, m, c], rs_recv.at[way, d - 1, m, c], device(-1 if way == UP else 1, 0, 0),
        )

    def send_sum(d, way, m, c, value):
        rs_out[way, d - 1, m * tok : (m + 1) * tok, chunks[c]] = value.astype(jnp.bfloat16)
        start(sum_copy(d, way, m, c))

    def side_sum(t):
        return remote(side_out.at[t], side_in.at[t], sx_send.at[t], sx_recv.at[t], device(0, -t, 0))

    def combine_side():
        for stage in range(STAGES):
            for q in range(2):
                if (stage, q) != (0, 0):
                    side_return(stage, q).wait_recv()
        for t in (2, 1, 3, 0):
            part = mix(mixing(side_info(t), "side", 2 * STAGE), side_ret[:, :, t].reshape(2 * STAGE, SIDE))
            if t:
                side_out[t] = part.astype(jnp.bfloat16)
                start(side_sum(t))
            else:
                side_own[...] = part

    for d in reversed(range(FAR + 1)):
        weights = {way: mixing(meta.at[stage_of(d, way)], "ring", STAGE) for way in ways(d)}
        for c in range(2):
            parts = {}
            for way in ways(d):
                stage = stage_of(d, way)
                returned(stage, c).wait_recv()
                parts[way] = mix(weights[way], ret[stage * STAGE : (stage + 1) * STAGE, chunks[c]])
            for m in range(micro):
                at = slice(m * tok, (m + 1) * tok)
                for way in ways(d):
                    mine = parts[way][at]
                    if d == FAR:
                        send_sum(d, c, m, c, mine)
                    elif d:
                        if d < FAR - 1 or c == way:
                            sum_copy(d + 1, way, m, c).wait_recv()
                            mine = mine + rs_in[way, d, at, chunks[c]].astype(jnp.float32)
                        send_sum(d, way, m, c, mine)
                    else:
                        for come in (UP, DOWN):
                            sum_copy(1, come, m, c).wait_recv()
                            mine = mine + rs_in[come, 0, at, chunks[c]].astype(jnp.float32)
                        result[m, :, chunks[c]] = mine.astype(jnp.bfloat16)
        if d == FAR - 1:
            combine_side()
        if d == 1:
            total = side_own[...]
            for t in range(1, ACROSS):
                side_sum(t).wait_recv()
                total = total + side_in[t].astype(jnp.float32)
            for m in range(micro):
                result[m, :, side] = total[m * tok : (m + 1) * tok].astype(jnp.bfloat16)
    out_copy = pltpu.make_async_copy(result, out_ref, out_sem)
    out_copy.start()

    for copy in sent:
        copy.wait_send()
    for stage in range(STAGES):
        for c in range(2):
            dispatched(stage, c).wait_send()
            returned(stage, c).wait_send()
    out_copy.wait()


def per_device(tokens, expert_ids, slot_ids, gate_values, gate_weight, up_weight, down_weight):
    micro, tok, width = tokens.shape
    hid = gate_weight.shape[2]
    bf16, f32, i32 = jnp.bfloat16, jnp.float32, jnp.int32
    anywhere = pl.BlockSpec(memory_space=pl.ANY)
    dma = pltpu.SemaphoreType.DMA
    slots, pair = STAGES * STAGE, micro * tok
    routes = [a.swapaxes(1, 2) for a in (expert_ids, slot_ids, gate_values)]
    return pl.pallas_call(
        kernel,
        out_shape=jax.ShapeDtypeStruct((micro, tok, width), bf16),
        in_specs=[anywhere] * 7,
        out_specs=anywhere,
        scratch_shapes=[
            pltpu.VMEM((width, hid), bf16),
            pltpu.VMEM((width, hid), bf16),
            pltpu.VMEM((hid, width), bf16),
            pltpu.VMEM((micro, 8, tok), i32),
            pltpu.VMEM((micro, 8, tok), i32),
            pltpu.VMEM((micro, 8, tok), f32),
            pltpu.VMEM((STAGES, pair, width), bf16),
            pltpu.VMEM((STAGES, micro, 16, 128), f32),
            pltpu.VMEM((slots, width), bf16),
            pltpu.VMEM((STAGES, ACROSS, 2, ROWS, width), bf16),
            pltpu.VMEM((slots, hid), bf16),
            pltpu.VMEM((STAGES, ACROSS, 2, ROWS, width), bf16),
            pltpu.VMEM((slots, width), bf16),
            pltpu.VMEM((2, FAR, pair, width), bf16),
            pltpu.VMEM((2, FAR, pair, width), bf16),
            pltpu.VMEM((micro, tok, width), bf16),
            pltpu.VMEM((ACROSS, pair, SIDE), bf16),
            pltpu.VMEM((ACROSS, micro, 16, 128), f32),
            pltpu.VMEM((STAGES, 2, ACROSS, ROWS, SIDE), bf16),
            pltpu.VMEM((STAGES, 2, ACROSS, ROWS, SIDE), bf16),
            pltpu.VMEM((ACROSS, pair, SIDE), bf16),
            pltpu.VMEM((ACROSS, pair, SIDE), bf16),
            pltpu.VMEM((pair, SIDE), f32),
            dma((3,)),
            dma((micro,)),
            dma((3,)),
            dma,
        ]
        + [dma((2, FAR))] * 2
        + [dma((2, FAR, micro, 2))] * 2
        + [dma((STAGES, 2))] * 4
        + [dma((2, FAR, micro, 2))] * 2
        + [dma((ACROSS,))] * 4
        + [dma((STAGES, 2))] * 4
        + [dma((ACROSS,))] * 2,
        compiler_params=pltpu.CompilerParams(
            collective_id=0, has_side_effects=True, vmem_limit_bytes=60 * 1024 * 1024
        ),
        cost_estimate=pl.CostEstimate(
            flops=2 * slots * 3 * width * hid,
            bytes_accessed=3 * width * hid * 2,
            transcendentals=slots * hid,
        ),
        name="experts",
    )(*routes, tokens, gate_weight, up_weight, down_weight)


def solution(mesh):
    tokens = P(None, ("dp", "ex", "ey"), None)
    weights = P(("ex", "ey"), None, None)
    return jax.shard_map(
        per_device,
        mesh=mesh,
        in_specs=(tokens,) * 4 + (weights,) * 3,
        out_specs=tokens,
        check_vma=False,
    )
```

```python
import jax
import jax.numpy as jnp
from jax import lax
from jax.experimental import pallas as pl
from jax.experimental.pallas import tpu as pltpu
from jax.sharding import PartitionSpec as P

MESH = pl.DeviceIdType.MESH
RING = 8
FAR = RING // 2
GROUP = 8
SLOTS = 8
ROWS = 2 * SLOTS
STAGE = GROUP * ROWS
UP, DOWN = 0, 1

STAGES = 8
STEPS = (0, 1, 7, 2, 6, 3, 5, 4)
FIRST = 5
EARLY = (3,)
SIDE = 256
ACROSS = GROUP // 2


def stage_of(d, way):
    return 0 if d == 0 else STAGES - 1 if d == FAR else 2 * d - 1 + way


def kernel(
    ids_ref, places_ref, gates_ref, tokens_ref, gate_ref, up_ref, down_ref, out_ref,
    wg, wu, wd, ids, places, gates, blocks, meta, spare, snd, rcv, hidden, answers, ret, rs_out, rs_in, result,
    side_blocks, side_meta, side_snd, side_ret, side_out, side_in, side_own,
    weight_sem, tok_sem, route_sem, out_sem,
    meta_send, meta_recv, ag_send, ag_recv, d_send, d_recv, r_send, r_recv, rs_send, rs_recv,
    sb_send, sb_recv, sm_send, sm_recv, sd_send, sd_recv, sr_send, sr_recv, sx_send, sx_recv,
):
    micro, tok, width = tokens_ref.shape
    pair = micro * tok
    middle = SIDE + (width - SIDE + 128) // 256 * 128
    chunks = [slice(SIDE, middle), slice(middle, width)]
    side = slice(0, SIDE)
    ex, ey = lax.axis_index("ex"), lax.axis_index("ey")
    z = ex // 2
    y = lax.rem(ex, 2) * 2 + ey // 2
    core = lax.rem(ey, 2)

    def device(dz, dy, dc):
        there_z = lax.rem(z + dz + RING, RING)
        there_y = lax.rem(y + dy + ACROSS, ACROSS)
        there_core = lax.rem(core + dc, 2)
        return {"ex": there_z * 2 + there_y // 2, "ey": lax.rem(there_y, 2) * 2 + there_core}

    def partner(r, back=False):
        return device(0, -(r // 2) if back else r // 2, r % 2)

    def remote(src, dst, send, recv, there):
        return pltpu.make_async_remote_copy(
            src_ref=src, dst_ref=dst, send_sem=send, recv_sem=recv, device_id=there, device_id_type=MESH
        )

    met = [partner(r) for r in range(1, GROUP)] + [device(1, 0, 0), device(-1, 0, 0)]
    barrier = pltpu.get_barrier_semaphore()
    for there in met:
        pl.semaphore_signal(barrier, inc=1, device_id=there, device_id_type=MESH)

    tok_copies = [
        pltpu.make_async_copy(tokens_ref.at[m], blocks.at[0, pl.ds(m * tok, tok)], tok_sem.at[m])
        for m in range(micro)
    ]
    route_copies = [
        pltpu.make_async_copy(src, dst, route_sem.at[i])
        for i, (src, dst) in enumerate(((ids_ref, ids), (places_ref, places), (gates_ref, gates)))
    ]
    weight_copies = [
        pltpu.make_async_copy(src.at[0], dst, weight_sem.at[i])
        for i, (src, dst) in enumerate(((gate_ref, wg), (up_ref, wu), (down_ref, wd)))
    ]
    for copy in tok_copies + route_copies + weight_copies:
        copy.start()

    lane = lax.broadcasted_iota(jnp.int32, (8, 128), 1)
    spare[...] = jnp.zeros_like(spare)
    for copy in route_copies:
        copy.wait()
    for m in range(micro):
        code = jnp.where(places[m] >= 0, ids[m] * SLOTS + places[m], -1)
        spare[m, 0:8, 0:tok] = code.astype(jnp.float32)
        spare[m, 8:16, 0:tok] = gates[m]
    for rows in (slice(0, 8), slice(8, 16)):
        meta[0, rows] = jnp.where(lane < tok, spare[0, rows], pltpu.roll(spare[1, rows], tok, 1))
    for copy in tok_copies:
        copy.wait()

    sent = []

    def start(copy):
        copy.start()
        sent.append(copy)

    def block_copy(d, way, m, c):
        at = pl.ds(m * tok, tok)
        return remote(
            blocks.at[stage_of(d, way), at, chunks[c]], blocks.at[stage_of(d + 1, way), at, chunks[c]],
            ag_send.at[way, d, m, c], ag_recv.at[way, d, m, c], device(1 - 2 * way, 0, 0),
        )

    def meta_copy(d, way):
        return remote(
            meta.at[stage_of(d, way)], meta.at[stage_of(d + 1, way)],
            meta_send.at[way, d], meta_recv.at[way, d], device(1 - 2 * way, 0, 0),
        )

    def pass_block(d, way, m, c):
        if d < FAR - 1 or c == way:
            start(block_copy(d, way, m, c))

    def pass_meta(d, way):
        if d < FAR - 1 or way == UP:
            start(meta_copy(d, way))

    def cells(info, mode):
        code = info[0:8, :].astype(jnp.int32)
        expert = code // SLOTS
        far, near = expert // GROUP, lax.rem(expert, GROUP)
        turn = lax.rem(near // 2 - y + ACROSS, ACROSS)
        other = lax.rem(near + core, 2)
        if mode == "side":
            u = lax.rem(far - z + RING, RING)
            stage = jnp.where(u == 0, 0, jnp.where(u < FAR, 2 * u - 1, jnp.where(u == FAR, 7, 2 * (RING - u))))
            good = turn == 0
            at = stage * 2 + other
        else:
            good = far == z
            at = turn * 2 + other
        at = at * ROWS + jnp.where(lane < tok, 0, SLOTS) + lax.rem(code, SLOTS)
        return jnp.where((code >= 0) & good & (lane < pair), at, -1)

    def select(info, mode, rows):
        where = cells(info, mode)
        row = lax.broadcasted_iota(jnp.int32, (rows, 128), 0)
        hit = row == where[0:1, :]
        for k in range(1, 8):
            hit = hit | (row == where[k : k + 1, :])
        return jnp.where(hit, 1.0, 0.0).astype(jnp.bfloat16)[:, 0:pair]

    def mixing(info, mode, rows):
        where = cells(info, mode)
        weight = info[8:16, :]
        row = lax.broadcasted_iota(jnp.int32, (rows, 128), 0)
        total = jnp.zeros((rows, 128), jnp.float32)
        for k in range(8):
            total = total + jnp.where(row == where[k : k + 1, :], weight[k : k + 1, :], 0.0)
        total = total.T[0:pair]
        high = total.astype(jnp.bfloat16)
        low = (total - high.astype(jnp.float32)).astype(jnp.bfloat16)
        return high, low

    def mix(weights, rows):
        high, low = weights
        return jnp.dot(high, rows, preferred_element_type=jnp.float32) + jnp.dot(
            low, rows, preferred_element_type=jnp.float32
        )

    def rows_of(stage, r, count=1):
        at = stage * STAGE + r * ROWS
        return pl.ds(at if isinstance(at, int) else pl.multiple_of(at, ROWS), count * ROWS)

    def all_rows(stage):
        return rows_of(stage, 1, GROUP - 1)

    soon = jnp.where(lax.rem(z, FAR) == 0, DOWN, UP)
    slow = jnp.where(lax.rem(z, FAR) == FAR - 1, DOWN, UP)

    def dispatched(stage, c):
        there = snd.at[all_rows(stage), chunks[c]]
        return remote(there, there, d_send.at[stage, c], d_recv.at[stage, c], device(0, 0, 0))

    def returned(stage, c):
        there = ret.at[all_rows(stage), chunks[c]]
        return remote(there, there, r_send.at[stage, c], r_recv.at[stage, c], device(0, 0, 0))

    def side_dispatch(stage, q):
        return remote(
            side_snd.at[stage, q], rcv.at[stage, :, q, :, side],
            sd_send.at[stage, q], sd_recv.at[stage, q], device(STEPS[stage], 0, q),
        )

    def side_return(stage, q):
        return remote(
            answers.at[stage, :, q, :, side], side_ret.at[stage, q],
            sr_send.at[stage, q], sr_recv.at[stage, q], device(-STEPS[stage], 0, q),
        )

    side_block_copies, side_meta_copies = {}, {}
    for t in range(1, ACROSS):
        side_block_copies[t] = remote(
            blocks.at[0, :, side], side_blocks.at[t], sb_send.at[t], sb_recv.at[t], device(0, t, 0)
        )
        side_meta_copies[t] = remote(meta.at[0], side_meta.at[t], sm_send.at[t], sm_recv.at[t], device(0, t, 0))

    def side_info(t):
        return side_meta.at[t] if t else meta.at[0]

    def choose(stage, c, choice):
        chosen = jnp.dot(
            choice, blocks[stage, :, chunks[c]], preferred_element_type=jnp.float32
        ).astype(jnp.bfloat16)
        rcv[stage, 0, 0, :, chunks[c]] = chosen[0:ROWS]
        snd[all_rows(stage), chunks[c]] = chosen[ROWS:STAGE]

    def dispatch(stage, c):
        for r in range(1, GROUP):
            remote(
                snd.at[rows_of(stage, r), chunks[c]], rcv.at[stage, r // 2, r % 2, :, chunks[c]],
                d_send.at[stage, c], d_recv.at[stage, c], partner(r),
            ).start()

    choice = select(meta.at[0], "ring", STAGE)
    for c in range(2):
        choose(0, c, choice)
    pl.semaphore_wait(barrier, len(met))
    for way in (UP, DOWN):
        pass_block(0, way, 0, 0)
        pass_meta(0, way)
    for t in (1, 3, 2):
        start(side_meta_copies[t])
        start(side_block_copies[t])
    for m, c in ((1, 0), (0, 1), (1, 1)):
        for way in (UP, DOWN):
            pass_block(0, way, m, c)
    for c in range(2):
        dispatch(0, c)

    def choose_side():
        for t in (0, 1, 3, 2):
            if t:
                side_meta_copies[t].wait_recv()
                side_block_copies[t].wait_recv()
            choice = select(side_info(t), "side", 2 * STAGE)
            tokens = side_blocks[t] if t else blocks[0, :, side]
            chosen = jnp.dot(choice, tokens, preferred_element_type=jnp.float32).astype(jnp.bfloat16)
            side_snd[:, :, t] = chosen.reshape(STAGES, 2, ROWS, SIDE)
        rcv[0, :, 0, :, side] = side_snd[0, 0]

    def dispatch_side(*stages):
        for stage in stages:
            for q in range(2):
                if (stage, q) != (0, 0):
                    start(side_dispatch(stage, q))

    def ways(d):
        return (UP, DOWN) if 0 < d < FAR else (UP,)

    def take(d, way, m, c):
        if d == FAR:
            block_copy(d - 1, c, m, c).wait_recv()
        else:
            block_copy(d - 1, way, m, c).wait_recv()
            pass_block(d, way, m, c)
        if (m, c) == (0, 0):
            meta_copy(d - 1, way).wait_recv()
            if d < FAR:
                pass_meta(d, way)

    def dispatch_step(d):
        choices = {}

        def place(i, way, c):
            stage = stage_of(d, way)
            if c == 0:
                choices[i] = select(meta.at[stage], "ring", STAGE)
            choose(stage, c, choices[i])
            dispatch(stage, c)

        for c in range(2):
            if d == 1:
                for i, way in enumerate((soon, 1 - soon)):
                    for m in range(micro):
                        take(d, way, m, c)
                    place(i, way, c)
            else:
                for m in range(micro):
                    for way in ways(d):
                        take(d, way, m, c)
                for i, way in enumerate(ways(d)):
                    place(i, way, c)

    up_tile, down_tile = 512, 1024

    def await_rows(first, last):
        for stage in range(first, last):
            for c in range(2):
                dispatched(stage, c).wait_recv()
            for q in range(2):
                if (stage, q) != (0, 0):
                    side_dispatch(stage, q).wait_recv()

    def expert_up(first, last):
        @pl.loop(0, wg.shape[1] // up_tile)
        def _(i):
            at = pl.ds(pl.multiple_of(i * up_tile, up_tile), up_tile)
            rows = rcv[first:last].reshape((last - first) * STAGE, width)
            gate_part = jnp.dot(rows, wg[:, at], preferred_element_type=jnp.float32)
            up_part = jnp.dot(rows, wu[:, at], preferred_element_type=jnp.float32)
            hidden[first * STAGE : last * STAGE, at] = (
                gate_part / (1.0 + jnp.exp(-gate_part)) * up_part
            ).astype(jnp.bfloat16)

    def expert_down(first, last):
        @pl.loop(0, width // down_tile)
        def _(i):
            at = pl.ds(pl.multiple_of(i * down_tile, down_tile), down_tile)
            answer = jnp.dot(
                hidden[first * STAGE : last * STAGE], wd[:, at], preferred_element_type=jnp.float32
            )
            answers[first:last, :, :, :, at] = answer.astype(jnp.bfloat16).reshape(
                last - first, ACROSS, 2, ROWS, down_tile
            )

    def give_back(stage, parts=(0, 1)):
        for c in parts:
            for r in range(1, GROUP):
                remote(
                    answers.at[stage, r // 2, r % 2, :, chunks[c]], ret.at[rows_of(stage, r), chunks[c]],
                    r_send.at[stage, c], r_recv.at[stage, c], partner(r, True),
                ).start()
            ret[rows_of(stage, 0), chunks[c]] = answers[stage, 0, 0, :, chunks[c]]

    def give_back_side(stage):
        for q in range(2):
            if (stage, q) == (0, 0):
                side_ret[0, 0] = answers[0, :, 0, :, side]
            else:
                start(side_return(stage, q))

    dispatch_step(1)
    dispatch_step(2)
    choose_side()
    dispatch_side(1, 2, 3, 4, 0)
    dispatch_step(3)
    dispatch_side(5, 6)
    for copy in weight_copies:
        copy.wait()
    await_rows(0, FIRST)
    expert_up(0, FIRST)
    dispatch_step(FAR)
    dispatch_side(7)
    expert_down(0, FIRST)
    for stage in EARLY:
        give_back(stage)
    for stage in range(FIRST):
        give_back_side(stage)
    await_rows(FIRST, STAGES)
    expert_up(FIRST, STAGES)
    expert_down(FIRST, STAGES)
    give_back(7)
    for other in range(FIRST, STAGES):
        give_back_side(other)
    for c in range(2):
        for stage in (5, 6):
            give_back(stage, (c,))
    give_back(4)
    for c in range(2):
        for way in (slow, 1 - slow):
            give_back(1 + way, (c,))
    give_back(0)

    def sum_copy(d, way, m, c):
        at = pl.ds(m * tok, tok)
        return remote(
            rs_out.at[way, d - 1, at, chunks[c]], rs_in.at[way, d - 1, at, chunks[c]],
            rs_send.at[way, d - 1, m, c], rs_recv.at[way, d - 1, m, c], device(2 * way - 1, 0, 0),
        )

    def send_sum(d, way, m, c, value):
        rs_out[way, d - 1, m * tok : (m + 1) * tok, chunks[c]] = value.astype(jnp.bfloat16)
        start(sum_copy(d, way, m, c))

    def side_sum(t):
        return remote(side_out.at[t], side_in.at[t], sx_send.at[t], sx_recv.at[t], device(0, -t, 0))

    def combine_side():
        for stage in range(STAGES):
            for q in range(2):
                if (stage, q) != (0, 0):
                    side_return(stage, q).wait_recv()
        for t in (2, 1, 3, 0):
            part = mix(mixing(side_info(t), "side", 2 * STAGE), side_ret[:, :, t].reshape(2 * STAGE, SIDE))
            if t:
                side_out[t] = part.astype(jnp.bfloat16)
                start(side_sum(t))
            else:
                side_own[...] = part

    for d in reversed(range(FAR + 1)):
        order = (slow, 1 - slow) if d == 1 else ways(d)
        weights = [mixing(meta.at[stage_of(d, way)], "ring", STAGE) for way in order]
        for c in range(2):
            for i, way in enumerate(order):
                stage = stage_of(d, way)
                returned(stage, c).wait_recv()
                part = mix(weights[i], ret[rows_of(stage, 0, GROUP), chunks[c]])
                for m in range(micro):
                    at = slice(m * tok, (m + 1) * tok)
                    mine = part[at]
                    if d == FAR:
                        send_sum(d, c, m, c, mine)
                    elif d:
                        if d < FAR - 1 or c == way:
                            sum_copy(d + 1, way, m, c).wait_recv()
                            mine = mine + rs_in[way, d, at, chunks[c]].astype(jnp.float32)
                        send_sum(d, way, m, c, mine)
                    else:
                        for come in (UP, DOWN):
                            sum_copy(1, come, m, c).wait_recv()
                            mine = mine + rs_in[come, 0, at, chunks[c]].astype(jnp.float32)
                        result[m, :, chunks[c]] = mine.astype(jnp.bfloat16)
        if d == FAR - 2:
            combine_side()
        if d == 1:
            total = side_own[...]
            for t in range(1, ACROSS):
                side_sum(t).wait_recv()
                total = total + side_in[t].astype(jnp.float32)
            for m in range(micro):
                result[m, :, side] = total[m * tok : (m + 1) * tok].astype(jnp.bfloat16)
    out_copy = pltpu.make_async_copy(result, out_ref, out_sem)
    out_copy.start()

    for copy in sent:
        copy.wait_send()
    for stage in range(STAGES):
        for c in range(2):
            dispatched(stage, c).wait_send()
            returned(stage, c).wait_send()
    out_copy.wait()


def per_device(tokens, expert_ids, slot_ids, gate_values, gate_weight, up_weight, down_weight):
    micro, tok, width = tokens.shape
    hid = gate_weight.shape[2]
    bf16, f32, i32 = jnp.bfloat16, jnp.float32, jnp.int32
    anywhere = pl.BlockSpec(memory_space=pl.ANY)
    dma = pltpu.SemaphoreType.DMA
    slots, pair = STAGES * STAGE, micro * tok
    routes = [a.swapaxes(1, 2) for a in (expert_ids, slot_ids, gate_values)]
    return pl.pallas_call(
        kernel,
        out_shape=jax.ShapeDtypeStruct((micro, tok, width), bf16),
        in_specs=[anywhere] * 7,
        out_specs=anywhere,
        scratch_shapes=[
            pltpu.VMEM((width, hid), bf16),
            pltpu.VMEM((width, hid), bf16),
            pltpu.VMEM((hid, width), bf16),
            pltpu.VMEM((micro, 8, tok), i32),
            pltpu.VMEM((micro, 8, tok), i32),
            pltpu.VMEM((micro, 8, tok), f32),
            pltpu.VMEM((STAGES, pair, width), bf16),
            pltpu.VMEM((STAGES, 16, 128), f32),
            pltpu.VMEM((micro, 16, 128), f32),
            pltpu.VMEM((slots, width), bf16),
            pltpu.VMEM((STAGES, ACROSS, 2, ROWS, width), bf16),
            pltpu.VMEM((slots, hid), bf16),
            pltpu.VMEM((STAGES, ACROSS, 2, ROWS, width), bf16),
            pltpu.VMEM((slots, width), bf16),
            pltpu.VMEM((2, FAR, pair, width), bf16),
            pltpu.VMEM((2, FAR, pair, width), bf16),
            pltpu.VMEM((micro, tok, width), bf16),
            pltpu.VMEM((ACROSS, pair, SIDE), bf16),
            pltpu.VMEM((ACROSS, 16, 128), f32),
            pltpu.VMEM((STAGES, 2, ACROSS, ROWS, SIDE), bf16),
            pltpu.VMEM((STAGES, 2, ACROSS, ROWS, SIDE), bf16),
            pltpu.VMEM((ACROSS, pair, SIDE), bf16),
            pltpu.VMEM((ACROSS, pair, SIDE), bf16),
            pltpu.VMEM((pair, SIDE), f32),
            dma((3,)),
            dma((micro,)),
            dma((3,)),
            dma,
        ]
        + [dma((2, FAR))] * 2
        + [dma((2, FAR, micro, 2))] * 2
        + [dma((STAGES, 2))] * 4
        + [dma((2, FAR, micro, 2))] * 2
        + [dma((ACROSS,))] * 4
        + [dma((STAGES, 2))] * 4
        + [dma((ACROSS,))] * 2,
        compiler_params=pltpu.CompilerParams(
            collective_id=0, has_side_effects=True, vmem_limit_bytes=60 * 1024 * 1024
        ),
        cost_estimate=pl.CostEstimate(
            flops=2 * slots * 3 * width * hid,
            bytes_accessed=3 * width * hid * 2,
            transcendentals=slots * hid,
        ),
        name="experts",
    )(*routes, tokens, gate_weight, up_weight, down_weight)


def solution(mesh):
    tokens = P(None, ("dp", "ex", "ey"), None)
    weights = P(("ex", "ey"), None, None)
    return jax.shard_map(
        per_device,
        mesh=mesh,
        in_specs=(tokens,) * 4 + (weights,) * 3,
        out_specs=tokens,
        check_vma=False,
    )
```

```python
import jax
import jax.numpy as jnp
from jax import lax
from jax.experimental import pallas as pl
from jax.experimental.pallas import tpu as pltpu
from jax.sharding import PartitionSpec as P

MESH = pl.DeviceIdType.MESH
RING = 8
FAR = RING // 2
GROUP = 8
SLOTS = 8
ROWS = 2 * SLOTS
STAGE = GROUP * ROWS
UP, DOWN = 0, 1

STAGES = 8
STEPS = (0, 1, 7, 2, 6, 3, 5, 4)
FIRST = 5
EARLY = (3,)
SIDE = 256
ACROSS = GROUP // 2


def stage_of(d, way):
    return 0 if d == 0 else STAGES - 1 if d == FAR else 2 * d - 1 + way


def kernel(
    ids_ref, places_ref, gates_ref, tokens_ref, gate_ref, up_ref, down_ref, out_ref,
    wg, wu, wd, ids, places, gates, blocks, meta, spare, snd, rcv, hidden, answers, ret, rs_out, rs_in, result,
    side_blocks, side_meta, side_snd, side_ret, side_out, side_in, side_own,
    weight_sem, tok_sem, route_sem, out_sem,
    meta_send, meta_recv, ag_send, ag_recv, d_send, d_recv, r_send, r_recv, rs_send, rs_recv,
    sb_send, sb_recv, sm_send, sm_recv, sd_send, sd_recv, sr_send, sr_recv, sx_send, sx_recv,
):
    micro, tok, width = tokens_ref.shape
    pair = micro * tok
    middle = SIDE + (width - SIDE + 128) // 256 * 128
    chunks = [slice(SIDE, middle), slice(middle, width)]
    side = slice(0, SIDE)
    ex, ey = lax.axis_index("ex"), lax.axis_index("ey")
    z = ex // 2
    y = lax.rem(ex, 2) * 2 + ey // 2
    core = lax.rem(ey, 2)

    def device(dz, dy, dc):
        there_z = lax.rem(z + dz + RING, RING)
        there_y = lax.rem(y + dy + ACROSS, ACROSS)
        there_core = lax.rem(core + dc, 2)
        return {"ex": there_z * 2 + there_y // 2, "ey": lax.rem(there_y, 2) * 2 + there_core}

    def partner(r, back=False):
        return device(0, -(r // 2) if back else r // 2, r % 2)

    def remote(src, dst, send, recv, there):
        return pltpu.make_async_remote_copy(
            src_ref=src, dst_ref=dst, send_sem=send, recv_sem=recv, device_id=there, device_id_type=MESH
        )

    met = [partner(r) for r in range(1, GROUP)] + [device(1, 0, 0), device(-1, 0, 0)]
    barrier = pltpu.get_barrier_semaphore()
    for there in met:
        pl.semaphore_signal(barrier, inc=1, device_id=there, device_id_type=MESH)

    tok_copies = [
        pltpu.make_async_copy(tokens_ref.at[m], blocks.at[0, pl.ds(m * tok, tok)], tok_sem.at[m])
        for m in range(micro)
    ]
    route_copies = [
        pltpu.make_async_copy(src, dst, route_sem.at[i])
        for i, (src, dst) in enumerate(((ids_ref, ids), (places_ref, places), (gates_ref, gates)))
    ]
    weight_copies = [
        pltpu.make_async_copy(src.at[0], dst, weight_sem.at[i])
        for i, (src, dst) in enumerate(((gate_ref, wg), (up_ref, wu), (down_ref, wd)))
    ]
    for copy in tok_copies + route_copies + weight_copies:
        copy.start()

    lane = lax.broadcasted_iota(jnp.int32, (8, 128), 1)
    spare[...] = jnp.zeros_like(spare)
    for copy in route_copies:
        copy.wait()
    for m in range(micro):
        code = jnp.where(places[m] >= 0, ids[m] * SLOTS + places[m], -1)
        spare[m, 0:8, 0:tok] = code.astype(jnp.float32)
        spare[m, 8:16, 0:tok] = gates[m]
    for rows in (slice(0, 8), slice(8, 16)):
        meta[0, rows] = jnp.where(lane < tok, spare[0, rows], pltpu.roll(spare[1, rows], tok, 1))
    for copy in tok_copies:
        copy.wait()

    sent = []

    def start(copy):
        copy.start()
        sent.append(copy)

    def block_copy(d, way, m, c):
        at = pl.ds(m * tok, tok)
        return remote(
            blocks.at[stage_of(d, way), at, chunks[c]], blocks.at[stage_of(d + 1, way), at, chunks[c]],
            ag_send.at[way, d, m, c], ag_recv.at[way, d, m, c], device(1 - 2 * way, 0, 0),
        )

    def meta_copy(d, way):
        return remote(
            meta.at[stage_of(d, way)], meta.at[stage_of(d + 1, way)],
            meta_send.at[way, d], meta_recv.at[way, d], device(1 - 2 * way, 0, 0),
        )

    def pass_block(d, way, m, c):
        if d < FAR - 1 or c == way:
            start(block_copy(d, way, m, c))

    def pass_meta(d, way):
        if d < FAR - 1 or way == UP:
            start(meta_copy(d, way))

    def cells(info, mode):
        code = info[0:8, :].astype(jnp.int32)
        expert = code // SLOTS
        far, near = expert // GROUP, lax.rem(expert, GROUP)
        turn = lax.rem(near // 2 - y + ACROSS, ACROSS)
        other = lax.rem(near + core, 2)
        if mode == "side":
            u = lax.rem(far - z + RING, RING)
            stage = jnp.where(u == 0, 0, jnp.where(u < FAR, 2 * u - 1, jnp.where(u == FAR, 7, 2 * (RING - u))))
            good = turn == 0
            at = stage * 2 + other
        else:
            good = far == z
            at = turn * 2 + other
        at = at * ROWS + jnp.where(lane < tok, 0, SLOTS) + lax.rem(code, SLOTS)
        return jnp.where((code >= 0) & good & (lane < pair), at, -1)

    def select(info, mode, rows):
        where = cells(info, mode)
        row = lax.broadcasted_iota(jnp.int32, (rows, 128), 0)
        hit = row == where[0:1, :]
        for k in range(1, 8):
            hit = hit | (row == where[k : k + 1, :])
        return jnp.where(hit, 1.0, 0.0).astype(jnp.bfloat16)[:, 0:pair]

    def mixing(info, mode, rows):
        where = cells(info, mode)
        weight = info[8:16, :]
        row = lax.broadcasted_iota(jnp.int32, (rows, 128), 0)
        total = jnp.zeros((rows, 128), jnp.float32)
        for k in range(8):
            total = total + jnp.where(row == where[k : k + 1, :], weight[k : k + 1, :], 0.0)
        total = total.T[0:pair]
        high = total.astype(jnp.bfloat16)
        low = (total - high.astype(jnp.float32)).astype(jnp.bfloat16)
        return high, low

    def mix(weights, rows):
        high, low = weights
        return jnp.dot(high, rows, preferred_element_type=jnp.float32) + jnp.dot(
            low, rows, preferred_element_type=jnp.float32
        )

    def rows_of(stage, r, count=1):
        at = stage * STAGE + r * ROWS
        return pl.ds(at if isinstance(at, int) else pl.multiple_of(at, ROWS), count * ROWS)

    def all_rows(stage):
        return rows_of(stage, 1, GROUP - 1)

    soon = jnp.where(lax.rem(z, FAR) == 0, DOWN, UP)
    slow = jnp.where(lax.rem(z, FAR) == FAR - 1, DOWN, UP)

    def dispatched(stage, c):
        there = snd.at[all_rows(stage), chunks[c]]
        return remote(there, there, d_send.at[stage, c], d_recv.at[stage, c], device(0, 0, 0))

    def returned(stage, c):
        there = ret.at[all_rows(stage), chunks[c]]
        return remote(there, there, r_send.at[stage, c], r_recv.at[stage, c], device(0, 0, 0))

    def side_dispatch(stage, q):
        return remote(
            side_snd.at[stage, q], rcv.at[stage, :, q, :, side],
            sd_send.at[stage, q], sd_recv.at[stage, q], device(STEPS[stage], 0, q),
        )

    def side_return(stage, q):
        return remote(
            answers.at[stage, :, q, :, side], side_ret.at[stage, q],
            sr_send.at[stage, q], sr_recv.at[stage, q], device(-STEPS[stage], 0, q),
        )

    side_block_copies, side_meta_copies = {}, {}
    for t in range(1, ACROSS):
        side_block_copies[t] = remote(
            blocks.at[0, :, side], side_blocks.at[t], sb_send.at[t], sb_recv.at[t], device(0, t, 0)
        )
        side_meta_copies[t] = remote(meta.at[0], side_meta.at[t], sm_send.at[t], sm_recv.at[t], device(0, t, 0))

    def side_info(t):
        return side_meta.at[t] if t else meta.at[0]

    def choose(stage, c, choice):
        chosen = jnp.dot(
            choice, blocks[stage, :, chunks[c]], preferred_element_type=jnp.float32
        ).astype(jnp.bfloat16)
        rcv[stage, 0, 0, :, chunks[c]] = chosen[0:ROWS]
        snd[all_rows(stage), chunks[c]] = chosen[ROWS:STAGE]

    def dispatch(stage, c):
        for r in range(1, GROUP):
            remote(
                snd.at[rows_of(stage, r), chunks[c]], rcv.at[stage, r // 2, r % 2, :, chunks[c]],
                d_send.at[stage, c], d_recv.at[stage, c], partner(r),
            ).start()

    choice = select(meta.at[0], "ring", STAGE)
    for c in range(2):
        choose(0, c, choice)
    pl.semaphore_wait(barrier, len(met))
    for way in (UP, DOWN):
        pass_block(0, way, 0, 0)
        pass_meta(0, way)
    for t in (1, 3, 2):
        start(side_meta_copies[t])
        start(side_block_copies[t])
    for m, c in ((1, 0), (0, 1), (1, 1)):
        for way in (UP, DOWN):
            pass_block(0, way, m, c)
    for c in range(2):
        dispatch(0, c)

    def choose_side():
        for t in (0, 1, 3, 2):
            if t:
                side_meta_copies[t].wait_recv()
                side_block_copies[t].wait_recv()
            choice = select(side_info(t), "side", 2 * STAGE)
            tokens = side_blocks[t] if t else blocks[0, :, side]
            chosen = jnp.dot(choice, tokens, preferred_element_type=jnp.float32).astype(jnp.bfloat16)
            side_snd[:, :, t] = chosen.reshape(STAGES, 2, ROWS, SIDE)
        rcv[0, :, 0, :, side] = side_snd[0, 0]

    def dispatch_side(*stages):
        for stage in stages:
            for q in range(2):
                if (stage, q) != (0, 0):
                    start(side_dispatch(stage, q))

    def ways(d):
        return (UP, DOWN) if 0 < d < FAR else (UP,)

    def take(d, way, m, c):
        if d == FAR:
            block_copy(d - 1, c, m, c).wait_recv()
        else:
            block_copy(d - 1, way, m, c).wait_recv()
            pass_block(d, way, m, c)
        if (m, c) == (0, 0):
            meta_copy(d - 1, way).wait_recv()
            if d < FAR:
                pass_meta(d, way)

    def dispatch_step(d):
        choices = {}

        def place(i, way, c):
            stage = stage_of(d, way)
            if c == 0:
                choices[i] = select(meta.at[stage], "ring", STAGE)
            choose(stage, c, choices[i])
            dispatch(stage, c)

        for c in range(2):
            if d == 1:
                for i, way in enumerate((soon, 1 - soon)):
                    for m in range(micro):
                        take(d, way, m, c)
                    place(i, way, c)
            else:
                for m in range(micro):
                    for way in ways(d):
                        take(d, way, m, c)
                for i, way in enumerate(ways(d)):
                    place(i, way, c)

    up_tile, down_tile = 512, 1024

    def await_rows(first, last):
        for stage in range(first, last):
            for c in range(2):
                dispatched(stage, c).wait_recv()
            for q in range(2):
                if (stage, q) != (0, 0):
                    side_dispatch(stage, q).wait_recv()

    def expert_up(first, last):
        @pl.loop(0, wg.shape[1] // up_tile)
        def _(i):
            at = pl.ds(pl.multiple_of(i * up_tile, up_tile), up_tile)
            rows = rcv[first:last].reshape((last - first) * STAGE, width)
            gate_part = jnp.dot(rows, wg[:, at], preferred_element_type=jnp.float32)
            up_part = jnp.dot(rows, wu[:, at], preferred_element_type=jnp.float32)
            hidden[first * STAGE : last * STAGE, at] = (
                gate_part / (1.0 + jnp.exp(-gate_part)) * up_part
            ).astype(jnp.bfloat16)

    def expert_down(first, last):
        @pl.loop(0, width // down_tile)
        def _(i):
            at = pl.ds(pl.multiple_of(i * down_tile, down_tile), down_tile)
            answer = jnp.dot(
                hidden[first * STAGE : last * STAGE], wd[:, at], preferred_element_type=jnp.float32
            )
            answers[first:last, :, :, :, at] = answer.astype(jnp.bfloat16).reshape(
                last - first, ACROSS, 2, ROWS, down_tile
            )

    def give_back(stage, parts=(0, 1)):
        for c in parts:
            for r in range(1, GROUP):
                remote(
                    answers.at[stage, r // 2, r % 2, :, chunks[c]], ret.at[rows_of(stage, r), chunks[c]],
                    r_send.at[stage, c], r_recv.at[stage, c], partner(r, True),
                ).start()
            ret[rows_of(stage, 0), chunks[c]] = answers[stage, 0, 0, :, chunks[c]]

    def give_back_side(stage):
        for q in range(2):
            if (stage, q) == (0, 0):
                side_ret[0, 0] = answers[0, :, 0, :, side]
            else:
                start(side_return(stage, q))

    dispatch_step(1)
    dispatch_step(2)
    choose_side()
    dispatch_side(1, 2, 3, 4, 0)
    dispatch_step(3)
    dispatch_side(5, 6)
    for copy in weight_copies:
        copy.wait()
    await_rows(0, FIRST)
    expert_up(0, FIRST)
    dispatch_step(FAR)
    dispatch_side(7)
    expert_down(0, FIRST)
    for stage in EARLY:
        give_back(stage)
    for stage in range(FIRST):
        give_back_side(stage)
    for first, last in ((FIRST, STAGES - 1), (STAGES - 1, STAGES)):
        await_rows(first, last)
        expert_up(first, last)
        expert_down(first, last)
    give_back(7)
    for other in range(FIRST, STAGES):
        give_back_side(other)
    for c in range(2):
        for stage in (5, 6):
            give_back(stage, (c,))
    give_back(4)
    for c in range(2):
        for way in (slow, 1 - slow):
            give_back(1 + way, (c,))
    give_back(0)

    def sum_copy(d, way, m, c):
        at = pl.ds(m * tok, tok)
        return remote(
            rs_out.at[way, d - 1, at, chunks[c]], rs_in.at[way, d - 1, at, chunks[c]],
            rs_send.at[way, d - 1, m, c], rs_recv.at[way, d - 1, m, c], device(2 * way - 1, 0, 0),
        )

    def send_sum(d, way, m, c, value):
        rs_out[way, d - 1, m * tok : (m + 1) * tok, chunks[c]] = value.astype(jnp.bfloat16)
        start(sum_copy(d, way, m, c))

    def side_sum(t):
        return remote(side_out.at[t], side_in.at[t], sx_send.at[t], sx_recv.at[t], device(0, -t, 0))

    def combine_side():
        for stage in range(STAGES):
            for q in range(2):
                if (stage, q) != (0, 0):
                    side_return(stage, q).wait_recv()
        for t in (2, 1, 3, 0):
            part = mix(mixing(side_info(t), "side", 2 * STAGE), side_ret[:, :, t].reshape(2 * STAGE, SIDE))
            if t:
                side_out[t] = part.astype(jnp.bfloat16)
                start(side_sum(t))
            else:
                side_own[...] = part

    for d in reversed(range(FAR + 1)):
        order = (slow, 1 - slow) if d == 1 else ways(d)
        weights = [mixing(meta.at[stage_of(d, way)], "ring", STAGE) for way in order]
        for c in range(2):
            for i, way in enumerate(order):
                stage = stage_of(d, way)
                returned(stage, c).wait_recv()
                part = mix(weights[i], ret[rows_of(stage, 0, GROUP), chunks[c]])
                for m in range(micro):
                    at = slice(m * tok, (m + 1) * tok)
                    mine = part[at]
                    if d == FAR:
                        send_sum(d, c, m, c, mine)
                    elif d:
                        if d < FAR - 1 or c == way:
                            sum_copy(d + 1, way, m, c).wait_recv()
                            mine = mine + rs_in[way, d, at, chunks[c]].astype(jnp.float32)
                        send_sum(d, way, m, c, mine)
                    else:
                        for come in (UP, DOWN):
                            sum_copy(1, come, m, c).wait_recv()
                            mine = mine + rs_in[come, 0, at, chunks[c]].astype(jnp.float32)
                        result[m, :, chunks[c]] = mine.astype(jnp.bfloat16)
        if d == FAR - 2:
            combine_side()
        if d == 1:
            total = side_own[...]
            for t in range(1, ACROSS):
                side_sum(t).wait_recv()
                total = total + side_in[t].astype(jnp.float32)
            for m in range(micro):
                result[m, :, side] = total[m * tok : (m + 1) * tok].astype(jnp.bfloat16)
    out_copy = pltpu.make_async_copy(result, out_ref, out_sem)
    out_copy.start()

    for copy in sent:
        copy.wait_send()
    for stage in range(STAGES):
        for c in range(2):
            dispatched(stage, c).wait_send()
            returned(stage, c).wait_send()
    out_copy.wait()


def per_device(tokens, expert_ids, slot_ids, gate_values, gate_weight, up_weight, down_weight):
    micro, tok, width = tokens.shape
    hid = gate_weight.shape[2]
    bf16, f32, i32 = jnp.bfloat16, jnp.float32, jnp.int32
    anywhere = pl.BlockSpec(memory_space=pl.ANY)
    dma = pltpu.SemaphoreType.DMA
    slots, pair = STAGES * STAGE, micro * tok
    routes = [a.swapaxes(1, 2) for a in (expert_ids, slot_ids, gate_values)]
    return pl.pallas_call(
        kernel,
        out_shape=jax.ShapeDtypeStruct((micro, tok, width), bf16),
        in_specs=[anywhere] * 7,
        out_specs=anywhere,
        scratch_shapes=[
            pltpu.VMEM((width, hid), bf16),
            pltpu.VMEM((width, hid), bf16),
            pltpu.VMEM((hid, width), bf16),
            pltpu.VMEM((micro, 8, tok), i32),
            pltpu.VMEM((micro, 8, tok), i32),
            pltpu.VMEM((micro, 8, tok), f32),
            pltpu.VMEM((STAGES, pair, width), bf16),
            pltpu.VMEM((STAGES, 16, 128), f32),
            pltpu.VMEM((micro, 16, 128), f32),
            pltpu.VMEM((slots, width), bf16),
            pltpu.VMEM((STAGES, ACROSS, 2, ROWS, width), bf16),
            pltpu.VMEM((slots, hid), bf16),
            pltpu.VMEM((STAGES, ACROSS, 2, ROWS, width), bf16),
            pltpu.VMEM((slots, width), bf16),
            pltpu.VMEM((2, FAR, pair, width), bf16),
            pltpu.VMEM((2, FAR, pair, width), bf16),
            pltpu.VMEM((micro, tok, width), bf16),
            pltpu.VMEM((ACROSS, pair, SIDE), bf16),
            pltpu.VMEM((ACROSS, 16, 128), f32),
            pltpu.VMEM((STAGES, 2, ACROSS, ROWS, SIDE), bf16),
            pltpu.VMEM((STAGES, 2, ACROSS, ROWS, SIDE), bf16),
            pltpu.VMEM((ACROSS, pair, SIDE), bf16),
            pltpu.VMEM((ACROSS, pair, SIDE), bf16),
            pltpu.VMEM((pair, SIDE), f32),
            dma((3,)),
            dma((micro,)),
            dma((3,)),
            dma,
        ]
        + [dma((2, FAR))] * 2
        + [dma((2, FAR, micro, 2))] * 2
        + [dma((STAGES, 2))] * 4
        + [dma((2, FAR, micro, 2))] * 2
        + [dma((ACROSS,))] * 4
        + [dma((STAGES, 2))] * 4
        + [dma((ACROSS,))] * 2,
        compiler_params=pltpu.CompilerParams(
            collective_id=0, has_side_effects=True, vmem_limit_bytes=60 * 1024 * 1024
        ),
        cost_estimate=pl.CostEstimate(
            flops=2 * slots * 3 * width * hid,
            bytes_accessed=3 * width * hid * 2,
            transcendentals=slots * hid,
        ),
        name="experts",
    )(*routes, tokens, gate_weight, up_weight, down_weight)


def solution(mesh):
    tokens = P(None, ("dp", "ex", "ey"), None)
    weights = P(("ex", "ey"), None, None)
    return jax.shard_map(
        per_device,
        mesh=mesh,
        in_specs=(tokens,) * 4 + (weights,) * 3,
        out_specs=tokens,
        check_vma=False,
    )
```

```python
import jax
import jax.numpy as jnp
from jax import lax
from jax.experimental import pallas as pl
from jax.experimental.pallas import tpu as pltpu
from jax.sharding import PartitionSpec as P

MESH = pl.DeviceIdType.MESH
RING = 8
FAR = RING // 2
GROUP = 8
SLOTS = 8
ROWS = 2 * SLOTS
STAGE = GROUP * ROWS
UP, DOWN = 0, 1

STAGES = 8
STEPS = (0, 1, 7, 2, 6, 3, 5, 4)
FIRST = 5
EARLY = (3,)
SIDE = 256
ACROSS = GROUP // 2


def stage_of(d, way):
    return 0 if d == 0 else STAGES - 1 if d == FAR else 2 * d - 1 + way


def kernel(
    ids_ref, places_ref, gates_ref, tokens_ref, gate_ref, up_ref, down_ref, out_ref,
    wg, wu, wd, ids, places, gates, blocks, meta, spare, snd, rcv, hidden, answers, ret, rs_out, rs_in, result,
    side_blocks, side_meta, side_snd, side_ret, side_out, side_in, side_own,
    weight_sem, tok_sem, route_sem, out_sem,
    meta_send, meta_recv, ag_send, ag_recv, d_send, d_recv, r_send, r_recv, rs_send, rs_recv,
    sb_send, sb_recv, sm_send, sm_recv, sd_send, sd_recv, sr_send, sr_recv, sx_send, sx_recv,
):
    micro, tok, width = tokens_ref.shape
    pair = micro * tok
    middle = SIDE + (width - SIDE + 128) // 256 * 128
    chunks = [slice(SIDE, middle), slice(middle, width)]
    side = slice(0, SIDE)
    ex, ey = lax.axis_index("ex"), lax.axis_index("ey")
    z = ex // 2
    y = lax.rem(ex, 2) * 2 + ey // 2
    core = lax.rem(ey, 2)

    def device(dz, dy, dc):
        there_z = lax.rem(z + dz + RING, RING)
        there_y = lax.rem(y + dy + ACROSS, ACROSS)
        there_core = lax.rem(core + dc, 2)
        return {"ex": there_z * 2 + there_y // 2, "ey": lax.rem(there_y, 2) * 2 + there_core}

    def partner(r, back=False):
        return device(0, -(r // 2) if back else r // 2, r % 2)

    def remote(src, dst, send, recv, there):
        return pltpu.make_async_remote_copy(
            src_ref=src, dst_ref=dst, send_sem=send, recv_sem=recv, device_id=there, device_id_type=MESH
        )

    met = [partner(r) for r in range(1, GROUP)] + [device(1, 0, 0), device(-1, 0, 0)]
    barrier = pltpu.get_barrier_semaphore()
    for there in met:
        pl.semaphore_signal(barrier, inc=1, device_id=there, device_id_type=MESH)

    tok_copies = [
        pltpu.make_async_copy(tokens_ref.at[m], blocks.at[0, pl.ds(m * tok, tok)], tok_sem.at[m])
        for m in range(micro)
    ]
    route_copies = [
        pltpu.make_async_copy(src, dst, route_sem.at[i])
        for i, (src, dst) in enumerate(((ids_ref, ids), (places_ref, places), (gates_ref, gates)))
    ]
    weight_copies = [
        pltpu.make_async_copy(src.at[0], dst, weight_sem.at[i])
        for i, (src, dst) in enumerate(((gate_ref, wg), (up_ref, wu), (down_ref, wd)))
    ]
    for copy in tok_copies + route_copies + weight_copies:
        copy.start()

    lane = lax.broadcasted_iota(jnp.int32, (8, 128), 1)
    spare[...] = jnp.zeros_like(spare)
    for copy in route_copies:
        copy.wait()
    for m in range(micro):
        code = jnp.where(places[m] >= 0, ids[m] * SLOTS + places[m], -1)
        spare[m, 0:8, 0:tok] = code.astype(jnp.float32)
        spare[m, 8:16, 0:tok] = gates[m]
    for rows in (slice(0, 8), slice(8, 16)):
        meta[0, rows] = jnp.where(lane < tok, spare[0, rows], pltpu.roll(spare[1, rows], tok, 1))
    for copy in tok_copies:
        copy.wait()

    sent = []

    def start(copy):
        copy.start()
        sent.append(copy)

    def block_copy(d, way, m, c):
        at = pl.ds(m * tok, tok)
        return remote(
            blocks.at[stage_of(d, way), at, chunks[c]], blocks.at[stage_of(d + 1, way), at, chunks[c]],
            ag_send.at[way, d, m, c], ag_recv.at[way, d, m, c], device(1 - 2 * way, 0, 0),
        )

    def meta_copy(d, way):
        return remote(
            meta.at[stage_of(d, way)], meta.at[stage_of(d + 1, way)],
            meta_send.at[way, d], meta_recv.at[way, d], device(1 - 2 * way, 0, 0),
        )

    def pass_block(d, way, m, c):
        if d < FAR - 1 or c == way:
            start(block_copy(d, way, m, c))

    def pass_meta(d, way):
        if d < FAR - 1 or way == UP:
            start(meta_copy(d, way))

    def cells(info, mode):
        code = info[0:8, :].astype(jnp.int32)
        expert = code // SLOTS
        far, near = expert // GROUP, lax.rem(expert, GROUP)
        turn = lax.rem(near // 2 - y + ACROSS, ACROSS)
        other = lax.rem(near + core, 2)
        if mode == "side":
            u = lax.rem(far - z + RING, RING)
            stage = jnp.where(u == 0, 0, jnp.where(u < FAR, 2 * u - 1, jnp.where(u == FAR, 7, 2 * (RING - u))))
            good = turn == 0
            at = stage * 2 + other
        else:
            good = far == z
            at = turn * 2 + other
        at = at * ROWS + jnp.where(lane < tok, 0, SLOTS) + lax.rem(code, SLOTS)
        return jnp.where((code >= 0) & good & (lane < pair), at, -1)

    def select(info, mode, rows):
        where = cells(info, mode)
        row = lax.broadcasted_iota(jnp.int32, (rows, 128), 0)
        hit = row == where[0:1, :]
        for k in range(1, 8):
            hit = hit | (row == where[k : k + 1, :])
        return jnp.where(hit, 1.0, 0.0).astype(jnp.bfloat16)[:, 0:pair]

    def mixing(info, mode, rows):
        where = cells(info, mode)
        weight = info[8:16, :]
        row = lax.broadcasted_iota(jnp.int32, (rows, 128), 0)
        total = jnp.zeros((rows, 128), jnp.float32)
        for k in range(8):
            total = total + jnp.where(row == where[k : k + 1, :], weight[k : k + 1, :], 0.0)
        total = total.T[0:pair]
        high = total.astype(jnp.bfloat16)
        low = (total - high.astype(jnp.float32)).astype(jnp.bfloat16)
        return high, low

    def mix(weights, rows):
        high, low = weights
        return jnp.dot(high, rows, preferred_element_type=jnp.float32) + jnp.dot(
            low, rows, preferred_element_type=jnp.float32
        )

    def rows_of(stage, r, count=1):
        at = stage * STAGE + r * ROWS
        return pl.ds(at if isinstance(at, int) else pl.multiple_of(at, ROWS), count * ROWS)

    def all_rows(stage):
        return rows_of(stage, 1, GROUP - 1)

    soon = jnp.where(lax.rem(z, FAR) == 0, DOWN, UP)
    slow = jnp.where(lax.rem(z, FAR) == FAR - 1, DOWN, UP)

    def dispatched(stage, c):
        there = snd.at[all_rows(stage), chunks[c]]
        return remote(there, there, d_send.at[stage, c], d_recv.at[stage, c], device(0, 0, 0))

    def returned(stage, c):
        there = ret.at[all_rows(stage), chunks[c]]
        return remote(there, there, r_send.at[stage, c], r_recv.at[stage, c], device(0, 0, 0))

    def side_dispatch(stage, q):
        return remote(
            side_snd.at[stage, q], rcv.at[stage, :, q, :, side],
            sd_send.at[stage, q], sd_recv.at[stage, q], device(STEPS[stage], 0, q),
        )

    def side_return(stage, q):
        return remote(
            answers.at[stage, :, q, :, side], side_ret.at[stage, q],
            sr_send.at[stage, q], sr_recv.at[stage, q], device(-STEPS[stage], 0, q),
        )

    side_block_copies, side_meta_copies = {}, {}
    for t in range(1, ACROSS):
        side_block_copies[t] = remote(
            blocks.at[0, :, side], side_blocks.at[t], sb_send.at[t], sb_recv.at[t], device(0, t, 0)
        )
        side_meta_copies[t] = remote(meta.at[0], side_meta.at[t], sm_send.at[t], sm_recv.at[t], device(0, t, 0))

    def side_info(t):
        return side_meta.at[t] if t else meta.at[0]

    def choose(stage, c, choice):
        chosen = jnp.dot(
            choice, blocks[stage, :, chunks[c]], preferred_element_type=jnp.float32
        ).astype(jnp.bfloat16)
        rcv[stage, 0, 0, :, chunks[c]] = chosen[0:ROWS]
        snd[all_rows(stage), chunks[c]] = chosen[ROWS:STAGE]

    def dispatch(stage, c):
        for r in range(1, GROUP):
            remote(
                snd.at[rows_of(stage, r), chunks[c]], rcv.at[stage, r // 2, r % 2, :, chunks[c]],
                d_send.at[stage, c], d_recv.at[stage, c], partner(r),
            ).start()

    choice = select(meta.at[0], "ring", STAGE)
    for c in range(2):
        choose(0, c, choice)
    pl.semaphore_wait(barrier, len(met))
    for way in (UP, DOWN):
        pass_block(0, way, 0, 0)
        pass_meta(0, way)
    for t in (1, 3, 2):
        start(side_meta_copies[t])
        start(side_block_copies[t])
    for m, c in ((1, 0), (0, 1), (1, 1)):
        for way in (UP, DOWN):
            pass_block(0, way, m, c)
    for c in range(2):
        dispatch(0, c)

    def choose_side():
        for t in (0, 1, 3, 2):
            if t:
                side_meta_copies[t].wait_recv()
                side_block_copies[t].wait_recv()
            choice = select(side_info(t), "side", 2 * STAGE)
            tokens = side_blocks[t] if t else blocks[0, :, side]
            chosen = jnp.dot(choice, tokens, preferred_element_type=jnp.float32).astype(jnp.bfloat16)
            side_snd[:, :, t] = chosen.reshape(STAGES, 2, ROWS, SIDE)
        rcv[0, :, 0, :, side] = side_snd[0, 0]

    def dispatch_side(*stages):
        for stage in stages:
            for q in range(2):
                if (stage, q) != (0, 0):
                    start(side_dispatch(stage, q))

    def ways(d):
        return (UP, DOWN) if 0 < d < FAR else (UP,)

    def take(d, way, m, c):
        if d == FAR:
            block_copy(d - 1, c, m, c).wait_recv()
        else:
            block_copy(d - 1, way, m, c).wait_recv()
            pass_block(d, way, m, c)
        if (m, c) == (0, 0):
            meta_copy(d - 1, way).wait_recv()
            if d < FAR:
                pass_meta(d, way)

    def dispatch_step(d):
        choices = {}

        def place(i, way, c):
            stage = stage_of(d, way)
            if c == 0:
                choices[i] = select(meta.at[stage], "ring", STAGE)
            choose(stage, c, choices[i])
            dispatch(stage, c)

        for c in range(2):
            if d == 1:
                for i, way in enumerate((soon, 1 - soon)):
                    for m in range(micro):
                        take(d, way, m, c)
                    place(i, way, c)
            else:
                for m in range(micro):
                    for way in ways(d):
                        take(d, way, m, c)
                for i, way in enumerate(ways(d)):
                    place(i, way, c)

    up_tile, down_tile = 512, 1024

    def await_rows(first, last):
        for stage in range(first, last):
            for c in range(2):
                dispatched(stage, c).wait_recv()
            for q in range(2):
                if (stage, q) != (0, 0):
                    side_dispatch(stage, q).wait_recv()

    def expert_up(first, last):
        @pl.loop(0, wg.shape[1] // up_tile)
        def _(i):
            at = pl.ds(pl.multiple_of(i * up_tile, up_tile), up_tile)
            rows = rcv[first:last].reshape((last - first) * STAGE, width)
            gate_part = jnp.dot(rows, wg[:, at], preferred_element_type=jnp.float32)
            up_part = jnp.dot(rows, wu[:, at], preferred_element_type=jnp.float32)
            hidden[first * STAGE : last * STAGE, at] = (
                gate_part / (1.0 + jnp.exp(-gate_part)) * up_part
            ).astype(jnp.bfloat16)

    def expert_down(first, last):
        @pl.loop(0, width // down_tile)
        def _(i):
            at = pl.ds(pl.multiple_of(i * down_tile, down_tile), down_tile)
            answer = jnp.dot(
                hidden[first * STAGE : last * STAGE], wd[:, at], preferred_element_type=jnp.float32
            )
            answers[first:last, :, :, :, at] = answer.astype(jnp.bfloat16).reshape(
                last - first, ACROSS, 2, ROWS, down_tile
            )

    def give_back(stage, parts=(0, 1)):
        for c in parts:
            for r in range(1, GROUP):
                remote(
                    answers.at[stage, r // 2, r % 2, :, chunks[c]], ret.at[rows_of(stage, r), chunks[c]],
                    r_send.at[stage, c], r_recv.at[stage, c], partner(r, True),
                ).start()
            ret[rows_of(stage, 0), chunks[c]] = answers[stage, 0, 0, :, chunks[c]]

    def give_back_side(stage):
        for q in range(2):
            if (stage, q) == (0, 0):
                side_ret[0, 0] = answers[0, :, 0, :, side]
            else:
                start(side_return(stage, q))

    dispatch_step(1)
    dispatch_step(2)
    choose_side()
    dispatch_side(1, 2, 3, 4, 0)
    dispatch_step(3)
    dispatch_side(5, 6)
    for copy in weight_copies:
        copy.wait()
    await_rows(0, 3)
    expert_up(0, 3)
    expert_down(0, 3)
    dispatch_step(FAR)
    dispatch_side(7)
    await_rows(3, FIRST)
    expert_up(3, FIRST)
    expert_down(3, FIRST)
    for stage in EARLY:
        give_back(stage)
    for stage in range(FIRST):
        give_back_side(stage)
    for first, last in ((FIRST, STAGES - 1), (STAGES - 1, STAGES)):
        await_rows(first, last)
        expert_up(first, last)
        expert_down(first, last)
    give_back(7)
    for other in range(FIRST, STAGES):
        give_back_side(other)
    for c in range(2):
        for stage in (5, 6):
            give_back(stage, (c,))
    give_back(4)
    for c in range(2):
        for way in (slow, 1 - slow):
            give_back(1 + way, (c,))
    give_back(0)

    def sum_copy(d, way, m, c):
        at = pl.ds(m * tok, tok)
        return remote(
            rs_out.at[way, d - 1, at, chunks[c]], rs_in.at[way, d - 1, at, chunks[c]],
            rs_send.at[way, d - 1, m, c], rs_recv.at[way, d - 1, m, c], device(2 * way - 1, 0, 0),
        )

    def send_sum(d, way, m, c, value):
        rs_out[way, d - 1, m * tok : (m + 1) * tok, chunks[c]] = value.astype(jnp.bfloat16)
        start(sum_copy(d, way, m, c))

    def side_sum(t):
        return remote(side_out.at[t], side_in.at[t], sx_send.at[t], sx_recv.at[t], device(0, -t, 0))

    def combine_side():
        for stage in range(STAGES):
            for q in range(2):
                if (stage, q) != (0, 0):
                    side_return(stage, q).wait_recv()
        for t in (2, 1, 3, 0):
            part = mix(mixing(side_info(t), "side", 2 * STAGE), side_ret[:, :, t].reshape(2 * STAGE, SIDE))
            if t:
                side_out[t] = part.astype(jnp.bfloat16)
                start(side_sum(t))
            else:
                side_own[...] = part

    for d in reversed(range(FAR + 1)):
        order = (slow, 1 - slow) if d == 1 else ways(d)
        weights = [mixing(meta.at[stage_of(d, way)], "ring", STAGE) for way in order]
        for c in range(2):
            for i, way in enumerate(order):
                stage = stage_of(d, way)
                returned(stage, c).wait_recv()
                part = mix(weights[i], ret[rows_of(stage, 0, GROUP), chunks[c]])
                for m in range(micro):
                    at = slice(m * tok, (m + 1) * tok)
                    mine = part[at]
                    if d == FAR:
                        send_sum(d, c, m, c, mine)
                    elif d:
                        if d < FAR - 1 or c == way:
                            sum_copy(d + 1, way, m, c).wait_recv()
                            mine = mine + rs_in[way, d, at, chunks[c]].astype(jnp.float32)
                        send_sum(d, way, m, c, mine)
                    else:
                        for come in (UP, DOWN):
                            sum_copy(1, come, m, c).wait_recv()
                            mine = mine + rs_in[come, 0, at, chunks[c]].astype(jnp.float32)
                        result[m, :, chunks[c]] = mine.astype(jnp.bfloat16)
        if d == FAR - 2:
            combine_side()
        if d == 1:
            total = side_own[...]
            for t in range(1, ACROSS):
                side_sum(t).wait_recv()
                total = total + side_in[t].astype(jnp.float32)
            for m in range(micro):
                result[m, :, side] = total[m * tok : (m + 1) * tok].astype(jnp.bfloat16)
    out_copy = pltpu.make_async_copy(result, out_ref, out_sem)
    out_copy.start()

    for copy in sent:
        copy.wait_send()
    for stage in range(STAGES):
        for c in range(2):
            dispatched(stage, c).wait_send()
            returned(stage, c).wait_send()
    out_copy.wait()


def per_device(tokens, expert_ids, slot_ids, gate_values, gate_weight, up_weight, down_weight):
    micro, tok, width = tokens.shape
    hid = gate_weight.shape[2]
    bf16, f32, i32 = jnp.bfloat16, jnp.float32, jnp.int32
    anywhere = pl.BlockSpec(memory_space=pl.ANY)
    dma = pltpu.SemaphoreType.DMA
    slots, pair = STAGES * STAGE, micro * tok
    routes = [a.swapaxes(1, 2) for a in (expert_ids, slot_ids, gate_values)]
    return pl.pallas_call(
        kernel,
        out_shape=jax.ShapeDtypeStruct((micro, tok, width), bf16),
        in_specs=[anywhere] * 7,
        out_specs=anywhere,
        scratch_shapes=[
            pltpu.VMEM((width, hid), bf16),
            pltpu.VMEM((width, hid), bf16),
            pltpu.VMEM((hid, width), bf16),
            pltpu.VMEM((micro, 8, tok), i32),
            pltpu.VMEM((micro, 8, tok), i32),
            pltpu.VMEM((micro, 8, tok), f32),
            pltpu.VMEM((STAGES, pair, width), bf16),
            pltpu.VMEM((STAGES, 16, 128), f32),
            pltpu.VMEM((micro, 16, 128), f32),
            pltpu.VMEM((slots, width), bf16),
            pltpu.VMEM((STAGES, ACROSS, 2, ROWS, width), bf16),
            pltpu.VMEM((slots, hid), bf16),
            pltpu.VMEM((STAGES, ACROSS, 2, ROWS, width), bf16),
            pltpu.VMEM((slots, width), bf16),
            pltpu.VMEM((2, FAR, pair, width), bf16),
            pltpu.VMEM((2, FAR, pair, width), bf16),
            pltpu.VMEM((micro, tok, width), bf16),
            pltpu.VMEM((ACROSS, pair, SIDE), bf16),
            pltpu.VMEM((ACROSS, 16, 128), f32),
            pltpu.VMEM((STAGES, 2, ACROSS, ROWS, SIDE), bf16),
            pltpu.VMEM((STAGES, 2, ACROSS, ROWS, SIDE), bf16),
            pltpu.VMEM((ACROSS, pair, SIDE), bf16),
            pltpu.VMEM((ACROSS, pair, SIDE), bf16),
            pltpu.VMEM((pair, SIDE), f32),
            dma((3,)),
            dma((micro,)),
            dma((3,)),
            dma,
        ]
        + [dma((2, FAR))] * 2
        + [dma((2, FAR, micro, 2))] * 2
        + [dma((STAGES, 2))] * 4
        + [dma((2, FAR, micro, 2))] * 2
        + [dma((ACROSS,))] * 4
        + [dma((STAGES, 2))] * 4
        + [dma((ACROSS,))] * 2,
        compiler_params=pltpu.CompilerParams(
            collective_id=0, has_side_effects=True, vmem_limit_bytes=60 * 1024 * 1024
        ),
        cost_estimate=pl.CostEstimate(
            flops=2 * slots * 3 * width * hid,
            bytes_accessed=3 * width * hid * 2,
            transcendentals=slots * hid,
        ),
        name="experts",
    )(*routes, tokens, gate_weight, up_weight, down_weight)


def solution(mesh):
    tokens = P(None, ("dp", "ex", "ey"), None)
    weights = P(("ex", "ey"), None, None)
    return jax.shard_map(
        per_device,
        mesh=mesh,
        in_specs=(tokens,) * 4 + (weights,) * 3,
        out_specs=tokens,
        check_vma=False,
    )
```
